128 devices in a mesh: fsdp: 8 (over y, z_hi), expert: 16 (over z_lo, x, core).
Axes of the slice: x: 4, y: 4, z: 4 (z_hi: 2, z_lo: 2; z = z_hi * 2 + z_lo), core: 2. Of those that a mesh axis runs over, the one named last changes fastest.
Arguments:
- tokens: bfloat16 [1024, 5120], P(('fsdp', 'expert')), may hold values from -6 to 6
- gate_scores: bfloat16 [1024, 6], P(('fsdp', 'expert')), may hold values from 0.049804688 to 0.59765625
- expert_ids: int32 [1024, 6], P(('fsdp', 'expert')), may hold values from 0 to 63, all different within a row; in each aligned block of 8 rows (0 to 7, 8 to 15, ...) at most 2 rows name the same one
- expert_gate: bfloat16 [128, 5120, 768], P(('fsdp', 'expert')), may hold values from -0.078125 to 0.078125
- expert_up: bfloat16 [128, 5120, 768], P(('fsdp', 'expert')), may hold values from -0.078125 to 0.078125
- expert_down: bfloat16 [128, 768, 5120], P(('fsdp', 'expert')), may hold values from -0.15625 to 0.15625
- shared_gate: bfloat16 [5120, 3072], P('expert', 'fsdp'), may hold values from -0.078125 to 0.078125
- shared_up: bfloat16 [5120, 3072], P('expert', 'fsdp'), may hold values from -0.078125 to 0.078125
- shared_down: bfloat16 [3072, 5120], P('fsdp', 'expert'), may hold values from -0.109375 to 0.109375
Outputs:
- mixed: bfloat16 [1024, 5120], P(('fsdp', 'expert'))
The draws below stay inside these ranges and needn't reach their ends.
Inputs may be any that keep to these rules, and one draw needn't show every extreme that they name: `expert_ids`: each row names 6 different experts. Within the 8 rows of one device no expert is named by more than 2 rows, a bound that some block reaches.
All inputs are finite; a program needn't handle non-finite values.
Results may differ from the reference program's by a relative error of at most 0.0053.
Values may be sent and summed in bfloat16 or wider, within the bound.
A program may use at most 128 MiB of HBM per device.

```python
import math
import jax
import jax.numpy as jnp
import numpy as np
from jax import lax

D = 5120
FF_E = 1536
FF_S = 3072
TOP = 6
TOK_DEV = 8
EXPERTS = 64
CAP_DEV = 2
TOKENS = 1024
N_FSDP = 8
N_EXPERT = 16


def level_of(stream_key, dims, shards, least, high):
    def one(axis_at, parts):
        draws = jax.random.uniform(jax.random.fold_in(jax.random.fold_in(stream_key, 6), axis_at), (parts,), jnp.float32, least / len(shards), high / len(shards))
        return jnp.repeat(jnp.exp(draws), dims[axis_at] // parts).reshape((-1,) + (1,) * (len(dims) - axis_at - 1))

    factor_of = one(*shards[0])
    for cut in shards[1:]:
        factor_of = factor_of * one(*cut)
    return factor_of


def assign_block(key, own, number, rows, count, top, bound, skew):
    sequence = jax.random.permutation(key, count)
    heavy_load, ordinary = portions_of(count, rows * top, bound, skew, True), portions_of(count, rows * top, bound, skew, False)
    places = jnp.arange(count)

    def named(lengths, offset_by):
        used = int((lengths > 0).sum())
        fixed = max(1, used // 4)
        moved = fixed + (places - fixed + offset_by * (used - fixed)) % max(1, count - fixed)
        return jnp.zeros((count,), jnp.int32).at[sequence[jnp.where(places < fixed, places, moved)]].set(jnp.asarray(lengths, jnp.int32))

    lengths = jnp.where(number % 4 == 0, named(heavy_load, number // 4), named(ordinary, number - number // 4 - 1))
    mixed = jax.random.permutation(jax.random.fold_in(own, 3), count)
    donor, receiver = mixed[0:count // 2 * 2:2], mixed[1:count // 2 * 2:2]
    margin = jnp.minimum(lengths[donor] - 1, bound - lengths[receiver]) // 2
    margin = jnp.where((donor == sequence[0]) | (receiver == sequence[0]) | (lengths[receiver] == 0), 0, jnp.maximum(margin, 0))
    moved = jax.random.randint(jax.random.fold_in(own, 4), (count // 2,), 0, 1 << 20) % (margin + 1)
    lengths = lengths.at[donor].add(-moved).at[receiver].add(moved)
    items = jnp.searchsorted(jnp.cumsum(lengths), jnp.arange(rows * top), side="right").astype(jnp.int32)
    grid = items.reshape(top, rows).T
    grid = grid[jax.random.permutation(jax.random.fold_in(own, 1), rows)]
    offset_by = jax.random.randint(jax.random.fold_in(own, 2), (rows, 1), 0, top)
    return jnp.take_along_axis(grid, (jnp.arange(top)[None, :] + offset_by) % top, axis=1)


def portions_of(count, total, reach, skew, full):
    weights = [(1 << 20) // math.isqrt(rank ** skew) + 1 for rank in range(1, count + 1)]
    largest = reach if full else min(reach, max(-(-total // count), total * weights[0] // sum(weights)))
    least = 1 if total - largest >= count - 1 else 0
    counts, surplus = [largest] + [least] * (count - 1), total - largest - least * (count - 1)
    while surplus > 0:
        candidates = [i for i in range(1, count) if counts[i] < largest] or [i for i in range(1, count) if counts[i] < reach]
        whole, budget = sum([weights[i] for i in candidates]), surplus
        for i in candidates:
            addition = min(reach - counts[i], max(1, budget * weights[i] // whole), surplus)
            counts[i] = counts[i] + addition
            surplus = surplus - addition
    return np.array(counts)


def gaussian(own_key, extent, scale, reach, shards=(), kind=jnp.bfloat16):
    drawn = scale * jax.random.normal(own_key, extent, jnp.float32)
    if shards:
        drawn = drawn * level_of(own_key, extent, shards, -0.22, 0.18)
    return jnp.clip(drawn, -reach, reach).astype(kind)


def setup_inputs(seed: int = 0) -> dict:
    splits = jax.random.split(jax.random.key(seed), 10)
    tokens = gaussian(splits[0], (TOKENS, D), 1.0, 6.0, ((0, 128),))
    gate_scores = jnp.clip(0.049804688 + 0.54785156 * jax.random.uniform(splits[1], (TOKENS, TOP), jnp.float32) ** level_of(splits[1], (TOKENS, TOP), ((0, 128),), -0.2, 0.2), 0.049804688, 0.59765625).astype(jnp.bfloat16)
    expert_ids_keys = jax.random.split(jax.random.fold_in(splits[2], 1), TOKENS // TOK_DEV)
    expert_ids_turns = jax.random.permutation(jax.random.fold_in(splits[2], 3), TOKENS // TOK_DEV)
    expert_ids = jax.vmap(lambda own, number: assign_block(jax.random.fold_in(splits[2], 2), own, number, TOK_DEV, EXPERTS, TOP, CAP_DEV, 1))(expert_ids_keys, expert_ids_turns).reshape((TOKENS, TOP))
    expert_gate = gaussian(splits[3], (2 * EXPERTS, D, FF_E // 2), D ** -0.5, 0.078125, ((0, 128),))
    expert_up = gaussian(splits[4], (2 * EXPERTS, D, FF_E // 2), D ** -0.5, 0.078125, ((0, 128),))
    expert_down = gaussian(splits[5], (2 * EXPERTS, FF_E // 2, D), FF_E ** -0.5, 0.15625, ((0, 128),))
    shared_gate = gaussian(splits[6], (D, FF_S), D ** -0.5, 0.078125, ((0, 16), (1, 8)))
    shared_up = gaussian(splits[7], (D, FF_S), D ** -0.5, 0.078125, ((0, 16), (1, 8)))
    shared_down = gaussian(splits[8], (FF_S, D), FF_S ** -0.5, 0.109375, ((0, 8), (1, 16)))
    return {"tokens": tokens, "gate_scores": gate_scores, "expert_ids": expert_ids, "expert_gate": expert_gate, "expert_up": expert_up, "expert_down": expert_down, "shared_gate": shared_gate, "shared_up": shared_up, "shared_down": shared_down}


def silu_product(row_data, w_gate, w_up):
    gate_act = jnp.dot(row_data, w_gate, preferred_element_type=jnp.float32)
    up_proj = jnp.dot(row_data, w_up, preferred_element_type=jnp.float32)
    return (jax.nn.silu(gate_act) * up_proj).astype(jnp.bfloat16)


def reference(tokens, gate_scores, expert_ids, expert_gate, expert_up, expert_down, shared_gate, shared_up, shared_down):
    row_cap = N_FSDP * N_EXPERT * CAP_DEV
    half_width = FF_E // 2
    gate_pairs = expert_gate.reshape(EXPERTS, 2, D, half_width)
    up_pairs = expert_up.reshape(EXPERTS, 2, D, half_width)
    down_pairs = expert_down.reshape(EXPERTS, 2, half_width, D)
    scores = gate_scores.astype(jnp.float32)

    def one_expert(summed, inputs):
        w_gate, w_up, w_down, expert_idx = inputs
        is_hit = expert_ids == expert_idx
        token_weight = jnp.sum(jnp.where(is_hit, scores, jnp.zeros_like(scores)), axis=1)
        present = jnp.any(is_hit, axis=1)
        hit_rows = jnp.nonzero(present, size=row_cap, fill_value=0)[0].astype(jnp.int32)
        hit_count = jnp.sum(present.astype(jnp.int32))
        is_valid = jnp.arange(row_cap, dtype=jnp.int32) < hit_count
        picked_weight = token_weight[hit_rows]
        row_weight = jnp.where(is_valid, picked_weight, jnp.zeros_like(picked_weight))
        row_data = tokens[hit_rows]
        expert_out = jnp.zeros((row_cap, D), jnp.float32)
        for half_idx in range(2):
            hidden = silu_product(row_data, w_gate[half_idx], w_up[half_idx])
            part_sum = jnp.dot(hidden, w_down[half_idx], preferred_element_type=jnp.float32)
            part_sum = lax.optimization_barrier(part_sum.astype(jnp.bfloat16))
            expert_out = expert_out + part_sum.astype(jnp.float32)
        summed = summed.at[hit_rows].add(expert_out * row_weight[:, None])
        return summed, None

    start_sum = jnp.zeros((tokens.shape[0], D), jnp.float32)
    expert_range = jnp.arange(EXPERTS, dtype=jnp.int32)
    routed, unused_out = lax.scan(one_expert, start_sum, (gate_pairs, up_pairs, down_pairs, expert_range))
    shared_hidden = silu_product(tokens, shared_gate, shared_up)
    shared_out = jnp.dot(shared_hidden, shared_down, preferred_element_type=jnp.float32)
    return (routed + shared_out).astype(jnp.bfloat16)
```

```python
import functools

import jax
import jax.numpy as jnp
from jax import lax
from jax.experimental import pallas as pl
from jax.experimental.pallas import tpu as pltpu
from jax.sharding import PartitionSpec as P

MESH = pl.DeviceIdType.MESH
BF, F32 = jnp.bfloat16, jnp.float32
D, EXT, WID = 5120, 256, 896
DX = D + EXT
HALF, SHF, WIN = 768, 384, 384
ORDERS = ((0, 1, 2), (1, 2, 0), (2, 0, 1))
TN, NT, NN = (((0,), (0,)), ((), ())), (((1,), (1,)), ((), ())), (((1,), (0,)), ((), ()))


def mm(a, b, dims=NN):
    return lax.dot_general(a, b, dims, preferred_element_type=F32)


def kernel(
    tok, ext, wg_h, wu_h, wd_h, sg, su, sd, out,
    T, stage, sib, wg, wu, wd, WS, WR, WA, HT, PM, CM, ag, au, H, RO, PS, PR,
    DB, RA, SA, RB, SB, RC, SD, SDR, SZ, SZR, SQ, SHR, SHA, FO,
    lsem, s_sib, s_ag, r_ag, s_fw, r_fw, s_w, r_w, s_h, r_h, s_sd, r_sd, s_q, r_q, s_p, r_p,
    s_rs, r_rs, s_f, r_f, s_rel, r_rel,
):
    f, e = lax.axis_index("fsdp"), lax.axis_index("expert")
    c = lax.rem(e, 2)
    y, x = f // 2, lax.rem(e // 2, 4)
    zh, zl = lax.rem(f, 2), e // 8
    pos = (y, zh * 2 + zl, x)
    chip = (y * 4 + pos[1]) * 4 + x
    mine = zl * 4 + x

    def dev(p, core):
        return (p[0] * 2 + p[1] // 2, (lax.rem(p[1], 2) * 4 + p[2]) * 2 + core)

    def peer(axis, dist):
        p = list(pos)
        p[axis] = lax.rem(p[axis] + dist, 4)
        return dev(p, c)

    def group(i):
        zz, xx = lax.rem(zl + i // 4, 2), lax.rem(x + i % 4, 4)
        return dev((y, zh * 2 + zz, xx), c), zz * 4 + xx

    def cols(g, core):
        return pl.ds(pl.multiple_of(g * 2 * WID + core * WID, 128), WID)

    sibling = dev(pos, 1 - c)

    def remote(src, dst, ss, rs, to):
        return pltpu.make_async_remote_copy(
            src_ref=src, dst_ref=dst, send_sem=ss, recv_sem=rs, device_id=to, device_id_type=MESH
        )

    pend = []

    def go(cp):
        cp.start()
        pend.append(cp)
        return cp

    loads = [
        pltpu.make_async_copy(wg_h.at[0], wg, lsem.at[0]),
        pltpu.make_async_copy(wu_h.at[0], wu, lsem.at[1]),
        pltpu.make_async_copy(wd_h.at[0], wd.at[:, pl.ds(0, D)], lsem.at[2]),
    ]
    barrier = pltpu.get_barrier_semaphore()
    partners = [peer(a, d) for a in range(3) for d in (1, 2, 3)]
    partners += [group(i)[0] for i in (5, 6, 7)] + [sibling]
    for to in partners:
        pl.semaphore_signal(barrier, inc=1, device_id=to, device_id_type=MESH)

    rows16 = lax.broadcasted_iota(jnp.int32, (16, 1), 0) // 8 == c
    v = tok[...].astype(F32)
    stage[:, pl.ds(0, D)] = jnp.where(rows16, jnp.concatenate([v, v], 0), 0.0).astype(BF)
    v = ext[...].astype(F32)
    stage[:, pl.ds(D, EXT)] = jnp.where(rows16, jnp.concatenate([v, v], 0), 0.0).astype(BF)
    wd[:, pl.ds(D, EXT)] = jnp.zeros((HALF, EXT), BF)
    pl.semaphore_wait(barrier, len(partners))
    cp = go(remote(stage, sib, s_sib.at[0], s_sib.at[1], sibling))
    for ld in loads:
        ld.start()
    cp.wait_recv()
    T[pos[0], pos[1], pos[2]] = stage[...] + sib[...]

    def view(ref, order, depth, col):
        ix = [slice(None)] * 3
        for a in order[depth:]:
            ix[a] = pos[a]
        return ref.at[ix[0], ix[1], ix[2], :, col]

    def from_view(ref, order, depth, dist, col):
        ix = [slice(None)] * 3
        for a in order[depth:]:
            ix[a] = pos[a]
        ix[order[depth]] = lax.rem(pos[order[depth]] + 4 - dist, 4)
        return ref.at[ix[0], ix[1], ix[2], :, col]

    sent = {}

    def ag_send(g, s):
        for d in (1, 2, 3):
            src = view(T, ORDERS[g], s, cols(g, c))
            sent[g, s, d] = go(
                remote(src, src, s_ag.at[g, s, d - 1], r_ag.at[g, s, d - 1], peer(ORDERS[g][s], d))
            )

    fwd = []

    def ag_recv(g, s):
        for d in (1, 2, 3):
            sent[g, s, d].wait_recv()
            part = from_view(T, ORDERS[g], s, d, cols(g, c))
            fwd.append(go(remote(part, part, s_fw.at[g, s, d - 1], r_fw.at[g, s, d - 1], sibling)))

    for g in range(3):
        ag_send(g, 0)

    k_at = lax.broadcasted_iota(jnp.int32, (320, WIN), 0)
    l_at = lax.broadcasted_iota(jnp.int32, (320, WIN), 1)
    shift = (l_at == k_at + 64 * c).astype(F32).astype(BF)
    wt = mm(sg[...], shift, TN).astype(BF)
    for j in range(8):
        WS[j, pl.ds(0, 48)] = wt[48 * j : 48 * j + 48]
    wt = mm(su[...], shift, TN).astype(BF)
    for j in range(8):
        WS[j, pl.ds(48, 48)] = wt[48 * j : 48 * j + 48]
    w_sent = []
    for i in range(1, 8):
        to, j = group(i)
        w_sent.append(go(remote(WS.at[j], WR.at[mine, c], s_w.at[i - 1], r_w.at[i - 1], to)))
    WR[mine, c] = WS[mine]
    sdp = mm(sd[...], shift).astype(BF)

    for s in (1, 2):
        for g in range(3):
            ag_recv(g, s - 1)
            ag_send(g, s)
    for cp in w_sent:
        cp.wait_recv()
    rel = go(remote(WR.at[:, c], WR.at[:, c], s_rel.at[0], r_rel.at[0], sibling))
    rel.wait_recv()
    for j in range(8):
        o = 640 * j
        WA[:, pl.ds(o, 256)] = WR[j, 0, :, pl.ds(0, 256)]
        WA[:, pl.ds(o + 256, 128)] = WR[j, 0, :, pl.ds(256, 128)] + WR[j, 1, :, pl.ds(0, 128)]
        WA[:, pl.ds(o + 384, 256)] = WR[j, 1, :, pl.ds(128, 256)]
    for g in range(3):
        ag_recv(g, 2)
    for cp in fwd:
        cp.wait_recv()

    def gate_up(i, acc):
        col = pl.ds(pl.multiple_of(i * 640, 128), 640)
        t = T[pl.ds(2 * c, 2), :, :, :, col].reshape(512, 640)
        return acc + mm(WA[:, col], t, NT)

    acc = lax.fori_loop(0, 8, gate_up, jnp.zeros((96, 512), F32))
    HT[c, mine] = (jax.nn.silu(acc[:48]) * acc[48:]).astype(BF)
    h_sent = []
    for i in range(1, 8):
        to, j = group(i)
        h_sent.append(go(remote(HT.at[c, mine], HT.at[c, mine], s_h.at[i - 1], r_h.at[i - 1], to)))

    info = T[:, :, :, :, pl.ds(D, 128)].reshape(1024, 128).astype(F32).T
    hit = (info[0:8] == chip.astype(F32)).astype(F32)
    weight = jnp.sum(hit * info[8:16], axis=0, keepdims=True)
    hit = jnp.sum(hit, axis=0, keepdims=True)
    lane = lax.broadcasted_iota(jnp.int32, (8, 1024), 1)
    run = jnp.broadcast_to(hit, (8, 1024))
    for b in range(10):
        run = run + jnp.where(lane >= (1 << b), pltpu.roll(run, 1 << b, 1), 0.0)
    place = run[0:1] - 1.0
    slot = lax.broadcasted_iota(jnp.int32, (256, 1024), 0).astype(F32)
    pm = jnp.where(slot == place, hit, 0.0)
    PM[...] = pm.astype(BF)
    CM[...] = (pm * weight).T.astype(BF)

    ag[...] = jnp.zeros_like(ag)
    au[...] = jnp.zeros_like(au)
    loads[0].wait()
    loads[1].wait()

    def routed_in(i, _):
        col = pl.ds(pl.multiple_of(i * 640, 128), 640)
        xs = mm(PM[...], T[:, :, :, :, col].reshape(1024, 640)).astype(BF)
        ag[...] += mm(xs, wg[col, :])
        au[...] += mm(xs, wu[col, :])
        return 0

    lax.fori_loop(0, 8, routed_in, 0)
    H[...] = (jax.nn.silu(ag[...]) * au[...]).astype(BF)

    for cp in h_sent:
        cp.wait_recv()
    rel = go(remote(HT.at[c], HT.at[c], s_rel.at[1], r_rel.at[1], sibling))

    loads[2].wait()
    p_sent = []
    for g in range(3):
        PS[g] = mm(H[...], wd[:, cols(g, 1 - c)]).astype(BF)
        p_sent.append(go(remote(PS.at[g], PR.at[g], s_p.at[g], r_p.at[g], sibling)))

    rel.wait_recv()
    for t in range(2):
        part = mm(HT[t].reshape(SHF, 512), sdp, TN).astype(BF)
        for k in range(2):
            SD[2 * t + k] = part[256 * k : 256 * k + 256]
    sd_sent = []
    for d in (1, 2, 3):
        at = lax.rem(y + d, 4)
        sd_sent.append(go(remote(SD.at[at], SDR.at[d - 1], s_sd.at[d - 1], r_sd.at[d - 1], peer(0, d))))

    for g in range(3):
        RO[g] = mm(H[...], wd[:, cols(g, c)]).astype(BF)
    rs = {}
    for g in range(3):
        p_sent[g].wait_recv()
        both = (RO[g].astype(F32) + PR[g].astype(F32)).astype(BF)
        for k in range(4):
            DB[g, k] = mm(CM[pl.ds(256 * k, 256)], both).astype(BF).reshape(4, 4, 16, WID)
        a = ORDERS[g][2]
        for d in (1, 2, 3):
            ix = [slice(None)] * 3
            ix[a] = lax.rem(pos[a] + d, 4)
            rs[g, 0, d] = go(
                remote(DB.at[g, ix[0], ix[1], ix[2]], RA.at[g, d - 1], s_rs.at[g, 0, d - 1], r_rs.at[g, 0, d - 1], peer(a, d))
            )

    for cp in sd_sent:
        cp.wait_recv()
    tot = SD[y].astype(F32)
    for d in range(3):
        tot = tot + SDR[d].astype(F32)
    tot = tot.astype(BF)
    SZ[0] = tot[:128]
    SZ[1] = tot[128:]
    z_sent = go(remote(SZ.at[1 - zh], SZR, s_sd.at[3], r_sd.at[3], peer(1, 2)))
    z_sent.wait_recv()
    SQ[...] = (SZ[zh].astype(F32) + SZR[...].astype(F32)).astype(BF).reshape(8, 16, WIN)
    q_sent = []
    for i in range(1, 8):
        to, j = group(i)
        q_sent.append(go(remote(SQ.at[j], SHR.at[mine, c], s_q.at[i - 1], r_q.at[i - 1], to)))
    SHR[mine, c] = SQ[mine]

    for g in range(3):
        for d in (1, 2, 3):
            rs[g, 0, d].wait_recv()
        a3, a2 = ORDERS[g][2], ORDERS[g][1]
        rest = [a for a in range(3) if a != a3]
        for k in range(4):
            ix = [slice(None)] * 3
            ix[a3] = pos[a3]
            ix[rest[0]] = k
            tot = DB[(g, *ix)].astype(F32)
            for d in range(3):
                tot = tot + RA[g, d, k].astype(F32)
            SA[g, k] = tot.astype(BF)
        first = rest[0] == a2
        for d in (1, 2, 3):
            at = lax.rem(pos[a2] + d, 4)
            src = SA.at[g, at] if first else SA.at[g, :, at]
            rs[g, 1, d] = go(remote(src, RB.at[g, d - 1], s_rs.at[g, 1, d - 1], r_rs.at[g, 1, d - 1], peer(a2, d)))
    for cp in q_sent:
        cp.wait_recv()
    rel2 = go(remote(SHR.at[:, c], SHR.at[:, c], s_rel.at[2], r_rel.at[2], sibling))
    for g in range(3):
        for d in (1, 2, 3):
            rs[g, 1, d].wait_recv()
        a3, a2, a1 = ORDERS[g][2], ORDERS[g][1], ORDERS[g][0]
        rest = [a for a in range(3) if a != a3]
        tot = (SA[g, pos[a2]] if rest[0] == a2 else SA[g, :, pos[a2]]).astype(F32)
        for d in range(3):
            tot = tot + RB[g, d].astype(F32)
        SB[g] = tot.astype(BF)
        for d in (1, 2, 3):
            at = lax.rem(pos[a1] + d, 4)
            rs[g, 2, d] = go(
                remote(SB.at[g, at], RC.at[g, d - 1], s_rs.at[g, 2, d - 1], r_rs.at[g, 2, d - 1], peer(a1, d))
            )
    rel2.wait_recv()
    SHA[...] = jnp.zeros_like(SHA)
    for j in range(8):
        for k in range(2):
            SHA[:, pl.ds(640 * j + 256 * k, WIN)] += SHR[j, k].astype(F32)
    f_sent = []
    for g in range(3):
        for d in (1, 2, 3):
            rs[g, 2, d].wait_recv()
        tot = SB[g, pos[ORDERS[g][0]]].astype(F32) + SHA[:, cols(g, c)]
        for d in range(3):
            tot = tot + RC[g, d].astype(F32)
        FO[:, cols(g, c)] = tot.astype(BF)
        f_sent.append(go(remote(FO.at[:, cols(g, c)], FO.at[:, cols(g, c)], s_f.at[g], r_f.at[g], sibling)))
    for cp in f_sent:
        cp.wait_recv()
    res = FO[:, pl.ds(0, D)].astype(F32)
    out[...] = jnp.where(c == 0, res[:8], res[8:]).astype(BF)
    for cp in pend:
        cp.wait_send()


def local(tokens, gate_scores, expert_ids, expert_gate, expert_up, expert_down, shared_gate, shared_up, shared_down):
    ids = expert_ids.astype(BF)
    ext = jnp.concatenate(
        [ids, jnp.full((8, 2), -1, BF), gate_scores, jnp.zeros((8, EXT - 14), BF)], axis=1
    )
    vm, hbm = pl.BlockSpec(memory_space=pltpu.VMEM), pl.BlockSpec(memory_space=pl.ANY)
    dma = pltpu.SemaphoreType.DMA
    return pl.pallas_call(
        kernel,
        out_shape=jax.ShapeDtypeStruct((8, D), BF),
        in_specs=[vm, vm, hbm, hbm, hbm, vm, vm, vm],
        out_specs=vm,
        scratch_shapes=[
            pltpu.VMEM((4, 4, 4, 16, DX), BF),
            pltpu.VMEM((16, DX), BF),
            pltpu.VMEM((16, DX), BF),
            pltpu.VMEM((D, HALF), BF),
            pltpu.VMEM((D, HALF), BF),
            pltpu.VMEM((HALF, DX), BF),
            pltpu.VMEM((8, 96, WIN), BF),
            pltpu.VMEM((8, 2, 96, WIN), BF),
            pltpu.VMEM((96, D), BF),
            pltpu.VMEM((2, 8, 48, 512), BF),
            pltpu.VMEM((256, 1024), BF),
            pltpu.VMEM((1024, 256), BF),
            pltpu.VMEM((256, HALF), F32),
            pltpu.VMEM((256, HALF), F32),
            pltpu.VMEM((256, HALF), BF),
            pltpu.VMEM((3, 256, WID), BF),
            pltpu.VMEM((3, 256, WID), BF),
            pltpu.VMEM((3, 256, WID), BF),
            pltpu.VMEM((3, 4, 4, 4, 16, WID), BF),
            pltpu.VMEM((3, 3, 4, 4, 16, WID), BF),
            pltpu.VMEM((3, 4, 4, 16, WID), BF),
            pltpu.VMEM((3, 3, 4, 16, WID), BF),
            pltpu.VMEM((3, 4, 16, WID), BF),
            pltpu.VMEM((3, 3, 16, WID), BF),
            pltpu.VMEM((4, 256, WIN), BF),
            pltpu.VMEM((3, 256, WIN), BF),
            pltpu.VMEM((2, 128, WIN), BF),
            pltpu.VMEM((128, WIN), BF),
            pltpu.VMEM((8, 16, WIN), BF),
            pltpu.VMEM((8, 2, 16, WIN), BF),
            pltpu.VMEM((16, DX), F32),
            pltpu.VMEM((16, DX), BF),
            dma((3,)),
            dma((2,)),
            dma((3, 3, 3)), dma((3, 3, 3)),
            dma((3, 3, 3)), dma((3, 3, 3)),
            dma((7,)), dma((7,)),
            dma((7,)), dma((7,)),
            dma((4,)), dma((4,)),
            dma((7,)), dma((7,)),
            dma((3,)), dma((3,)),
            dma((3, 3, 3)), dma((3, 3, 3)),
            dma((3,)), dma((3,)),
            dma((3,)), dma((3,)),
        ],
        compiler_params=pltpu.CompilerParams(
            collective_id=0, has_side_effects=True, vmem_limit_bytes=62 * 2**20
        ),
        cost_estimate=pl.CostEstimate(flops=13 * 10**9, bytes_accessed=25 * 10**6, transcendentals=10**6),
    )(tokens, ext, expert_gate, expert_up, expert_down, shared_gate, shared_up, shared_down)


def solution(mesh):
    return jax.shard_map(
        local,
        mesh=mesh,
        in_specs=(
            P(("fsdp", "expert"), None),
            P(("fsdp", "expert"), None),
            P(("fsdp", "expert"), None),
            P(("fsdp", "expert"), None, None),
            P(("fsdp", "expert"), None, None),
            P(("fsdp", "expert"), None, None),
            P("expert", "fsdp"),
            P("expert", "fsdp"),
            P("fsdp", "expert"),
        ),
        out_specs=P(("fsdp", "expert"), None),
        check_vma=False,
    )
```

```python
import jax
import jax.numpy as jnp
from jax import lax
from jax.experimental import pallas as pl
from jax.experimental.pallas import tpu as pltpu
from jax.sharding import PartitionSpec as P

MESH = pl.DeviceIdType.MESH
BF, F32 = jnp.bfloat16, jnp.float32
D, HALF_D, HALF, WIN = 5120, 2560, 768, 384
ORDERS = ((0, 1, 2), (1, 2, 0), (2, 0, 1))
OFF, WIDTH = (0, 896, 1792), (896, 896, 768)
DAY = (256, 64, 16)
NN, TN, NT = (((1,), (0,)), ((), ())), (((0,), (0,)), ((), ())), (((1,), (1,)), ((), ()))


def mm(a, b, dims=NN):
    return lax.dot_general(a, b, dims, preferred_element_type=F32)


def running(v, width):
    lane = lax.broadcasted_iota(jnp.int32, v.shape, 1)
    step = 1
    while step < width:
        v = v + jnp.where(lane >= step, pltpu.roll(v, step, 1), 0.0)
        step *= 2
    return v


def kernel(
    tok, gates, ids, wg_h, wu_h, wd_h, sg_h, su_h, sd_h, out,
    T, ID, stage, sib, e8, idst, idsib, wg, wu, wd, sg, su, sd, WS, WR, WA, SPS, SPR, SPO, HT,
    PM, GM, CT, XO, XR, ag, au, H, RO, PS, PR, XC, RA, SA, RB, SB, RC, SD, SDR, SZ, SZR, SQ, SHR, SHA, FO,
    lsem, s_sib, r_sib, s_id, r_id, s_a0, r_a0, s_a1, r_a1, s_a2, r_a2, s_w, r_w, s_sp, r_sp, s_x, r_x,
    s_h, r_h, s_rel, r_rel, s_p, r_p, s_sd, r_sd, s_q, r_q, s_rs, r_rs, s_f, r_f,
):
    f, e = lax.axis_index("fsdp"), lax.axis_index("expert")
    c = lax.rem(e, 2)
    y, x = f // 2, lax.rem(e // 2, 4)
    zh, zl = lax.rem(f, 2), e // 8
    pos = (y, zh * 2 + zl, x)
    chip = (y * 4 + pos[1]) * 4 + x
    mine = zl * 4 + x

    def dev(p, core):
        return (p[0] * 2 + p[1] // 2, (lax.rem(p[1], 2) * 4 + p[2]) * 2 + core)

    def peer(axis, dist):
        p = list(pos)
        p[axis] = lax.rem(p[axis] + dist, 4)
        return dev(p, c)

    def group(i):
        zz, xx = lax.rem(zl + i // 4, 2), lax.rem(x + i % 4, 4)
        return dev((y, zh * 2 + zz, xx), c), zz * 4 + xx

    def taker(i):
        zz, xx = lax.rem(zl + i // 4, 2), lax.rem(x + i % 4, 4)
        return dev((y, zh * 2 + zz, xx), zl), zz * 4 + xx

    def giver(i):
        return dev((y, zh * 2 + c, lax.rem(x + i % 4, 4)), lax.rem(c + i // 4, 2))

    sibling = dev(pos, 1 - c)

    def half(core, off, width):
        return pl.ds(pl.multiple_of(core * HALF_D + off, 128), width)

    def remote(src, dst, ss, rs, to):
        return pltpu.make_async_remote_copy(
            src_ref=src, dst_ref=dst, send_sem=ss, recv_sem=rs, device_id=to, device_id_type=MESH
        )

    pend = []

    def go(src, dst, ss, rs, to):
        cp = remote(src, dst, ss, rs, to)
        cp.start()
        pend.append(cp)
        return cp

    loads = [
        pltpu.make_async_copy(a, b, lsem.at[i])
        for i, (a, b) in enumerate(
            ((sg_h, sg), (su_h, su), (sd_h, sd), (wg_h.at[0], wg), (wu_h.at[0], wu), (wd_h.at[0], wd))
        )
    ]
    barrier = pltpu.get_barrier_semaphore()
    partners = [peer(a, d) for a in range(3) for d in (1, 2, 3)]
    partners += [group(i)[0] for i in (5, 6, 7)] + [sibling] + [giver(i) for i in range(1, 8)]
    for to in partners:
        pl.semaphore_signal(barrier, inc=1, device_id=to, device_id_type=MESH)

    @pl.when(zl != c)
    def _():
        pl.semaphore_signal(barrier, inc=1, device_id=giver(0), device_id_type=MESH)

    for ld in loads:
        ld.start()

    rows16 = lax.broadcasted_iota(jnp.int32, (16, 1), 0) // 8 == c
    v = tok[...].astype(F32)
    stage[...] = jnp.where(rows16, jnp.concatenate([v, v], 0), 0.0).astype(BF)
    e8[...] = jnp.full((8, 128), -1.0, F32)
    e8[:, pl.ds(0, 6)] = ids[...].astype(F32)
    e8[:, pl.ds(8, 6)] = gates[...].astype(F32)
    v = e8[...]
    idst[...] = jnp.where(rows16, jnp.concatenate([v, v], 0), 0.0).astype(BF)
    pl.semaphore_wait(barrier, len(partners) + jnp.where(zl != c, 1, 0))

    cp = go(idst, idsib, s_sib.at[0], r_sib.at[0], sibling)
    cp1 = go(stage.at[:, half(1 - c, 0, HALF_D)], sib, s_sib.at[1], r_sib.at[1], sibling)

    def view(ref, order, depth, col):
        ix = [slice(None)] * 3
        for a in order[depth:]:
            ix[a] = pos[a]
        return ref.at[ix[0], ix[1], ix[2], :, col]

    def id_send(s):
        v = view(ID, (0, 1, 2), s, slice(None))
        return [go(v, v, s_id.at[s, d - 1], r_id.at[s, d - 1], peer(s, d)) for d in (1, 2, 3)]

    cp.wait_recv()
    ID[pos[0], pos[1], pos[2]] = idst[...] + idsib[...]
    id_cp = id_send(0)
    cp1.wait_recv()
    T[pos[0], pos[1], pos[2]] = stage[:, half(c, 0, HALF_D)] + sib[...]

    a0, a1, a2 = {}, {}, {}
    for g in range(3):
        v = view(T, ORDERS[g], 0, pl.ds(OFF[g], WIDTH[g]))
        for d in (1, 3, 2):
            a0[g, d] = go(v, v, s_a0.at[g, d - 1], r_a0.at[g, d - 1], peer(ORDERS[g][0], d))

    def piece(g, k, back, part):
        b1, b2, b3 = ORDERS[g]
        cut = 128 * ((WIDTH[g] // 128 + 1 - k % 2) // 2)
        ix = [slice(None)] * 3
        ix[b2] = lax.rem(pos[b2] + 4 - k, 4)
        ix[b3] = lax.rem(pos[b3] + 4 - back, 4)
        col = pl.ds(OFF[g], cut) if part == 0 else pl.ds(OFF[g] + cut, WIDTH[g] - cut)
        return T.at[ix[0], ix[1], ix[2], :, col]

    def third(g, k, j):
        back, part, way = ((0, 0, 1), (0, 1, 3), (0, 1, 1), (0, 0, 3), (1, 0, 1), (3, 1, 3))[j]
        v = piece(g, k, back, part)
        a2[g, k, j] = go(v, v, s_a2.at[g, k, j], r_a2.at[g, k, j], peer(ORDERS[g][2], way))

    def slab(g, k):
        for j in range(4):
            third(g, k, j)

    def pass_on(k):
        for g in range(3):
            for j in (0, 1):
                a2[g, k, j].wait_recv()
                third(g, k, j + 4)

    for ld in loads[:3]:
        ld.wait()
    k_at = lax.broadcasted_iota(jnp.int32, (320, WIN), 0)
    l_at = lax.broadcasted_iota(jnp.int32, (320, WIN), 1)
    shift = (l_at == k_at + 64 * c).astype(F32).astype(BF)
    wt = mm(sg[...], shift, TN).astype(BF)
    for j in range(8):
        WS[j, pl.ds(0, 48)] = wt[48 * j : 48 * j + 48]
    wt = mm(su[...], shift, TN).astype(BF)
    for j in range(8):
        WS[j, pl.ds(48, 48)] = wt[48 * j : 48 * j + 48]

    def spread(src, dst, ss, rs):
        for i in range(1, 8):
            to, j = taker(i)
            go(src.at[j], dst.at[x, c], ss.at[i], rs.at[i % 4, c], to)

        @pl.when(zl != c)
        def _():
            to, j = taker(0)
            remote(src.at[j], dst.at[x, c], ss.at[0], rs.at[0, c], to).start()

        @pl.when(zl == c)
        def _():
            dst[x, c] = src[mine]

    def spread_recv(dst, rs):
        for i in range(1, 8):
            cc = lax.rem(c + i // 4, 2)
            pltpu.make_async_copy(dst.at[0, 0], dst.at[0, 0], rs.at[i % 4, cc]).wait()

        @pl.when(zl != c)
        def _():
            pltpu.make_async_copy(dst.at[0, 0], dst.at[0, 0], rs.at[0, c]).wait()

    def spread_end(src, ss):
        @pl.when(zl != c)
        def _():
            pltpu.make_async_copy(src.at[0], src.at[0], ss.at[0]).wait()

    spread(WS, WR, s_w, r_w)
    sdp = mm(sd[...], shift, TN).astype(BF)

    for cp in id_cp:
        cp.wait_recv()
    id_cp = id_send(1)
    for g in range(3):
        for d in (1, 3, 2):
            a0[g, d].wait_recv()
        v = view(T, ORDERS[g], 1, pl.ds(OFF[g], WIDTH[g]))
        for d in (1, 3, 2):
            a1[g, d] = go(v, v, s_a1.at[g, d - 1], r_a1.at[g, d - 1], peer(ORDERS[g][1], d))
    for g in range(3):
        slab(g, 0)
    for cp in id_cp:
        cp.wait_recv()
    id_cp = id_send(2)
    last = 0
    for k in (1, 3, 2):
        for g in range(3):
            a1[g, k].wait_recv()
            slab(g, k)
        pass_on(last)
        last = k
    pass_on(last)

    for cp in id_cp:
        cp.wait_recv()
    info = ID[...].reshape(1024, 128).astype(F32).T
    at = lax.broadcasted_iota(jnp.int32, (1, 1024), 1)
    hit = jnp.sum((info[0:8] == chip.astype(F32)).astype(F32), axis=0, keepdims=True)
    plane = [
        jnp.where(lax.rem(at // DAY[ORDERS[g][2]], 4) == p, hit, 0.0) for g in range(3) for p in range(4)
    ]
    run = running(jnp.concatenate(plane + [hit] * 4, 0), 1024) - 1.0
    slot = lax.broadcasted_iota(jnp.int32, (256, 1024), 0).astype(F32)
    PM[...] = jnp.where(slot == run[12:13], hit, 0.0).astype(BF)
    slot = lax.broadcasted_iota(jnp.int32, (64, 1024), 0).astype(F32)
    for g in range(3):
        pick = [jnp.where(slot == run[4 * g + p : 4 * g + p + 1], plane[4 * g + p], 0.0) for p in range(4)]
        GM[g] = mm(jnp.concatenate(pick, 0).astype(BF), PM[...], NT).astype(BF)
    slot = lax.broadcasted_iota(jnp.int32, (64, 256), 0).astype(F32)
    for g in range(3):
        b3 = ORDERS[g][2]
        ix = [slice(None)] * 3
        ix[b3] = pos[b3]
        info = ID[ix[0], ix[1], ix[2]].reshape(256, 128).astype(F32).T
        hits, weights = [], []
        for d in range(4):
            p = list(pos)
            p[b3] = lax.rem(p[b3] + 4 - d, 4)
            eq = (info[0:8] == ((p[0] * 4 + p[1]) * 4 + p[2]).astype(F32)).astype(F32)
            hits.append(jnp.sum(eq, axis=0, keepdims=True))
            weights.append(jnp.sum(eq * info[8:16], axis=0, keepdims=True))
        run = running(jnp.concatenate(hits + hits, 0), 256) - 1.0
        for d in range(4):
            CT[g, pl.ds(64 * d, 64)] = jnp.where(
                slot == run[d : d + 1], weights[d] * hits[d], 0.0
            ).astype(BF)

    spread_recv(WR, r_w)
    for j in range(4):
        o = 640 * j
        WA[:, pl.ds(o, 256)] = WR[j, 0, :, pl.ds(0, 256)]
        WA[:, pl.ds(o + 256, 128)] = WR[j, 0, :, pl.ds(256, 128)] + WR[j, 1, :, pl.ds(0, 128)]
        WA[:, pl.ds(o + 384, 256)] = WR[j, 1, :, pl.ds(128, 256)]
    for k in (0, 1, 3, 2):
        for g in range(3):
            for j in (2, 3, 4, 5):
                a2[g, k, j].wait_recv()

    def gate_up(core):
        def step(i, acc):
            col = pl.ds(pl.multiple_of(i * 640, 128), 640)
            return acc + mm(WA[:, col], T[pl.ds(2 * core, 2), :, :, :, col].reshape(512, 640), NT)

        return lax.fori_loop(0, 4, step, jnp.zeros((96, 512), F32))

    SPS[...] = gate_up(1 - c)
    sp = go(SPS, SPR, s_sp.at[0], r_sp.at[0], sibling)
    SPO[...] = gate_up(c)

    x_cp = []
    for i in range(4):
        col = pl.ds(640 * i, 640)
        XO[i] = mm(PM[...], T[:, :, :, :, col].reshape(1024, 640)).astype(BF)
        x_cp.append(go(XO.at[i], XR.at[i], s_x.at[i], r_x.at[i], sibling))

    sp.wait_recv()
    gu = SPO[...] + SPR[...]
    HT[c, mine] = (jax.nn.silu(gu[:48]) * gu[48:]).astype(BF)
    h_cp = []
    for i in range(1, 8):
        to, j = group(i)
        h_cp.append(go(HT.at[c, mine], HT.at[c, mine], s_h.at[i - 1], r_h.at[i - 1], to))

    loads[3].wait()
    loads[4].wait()
    ag[...] = jnp.zeros_like(ag)
    au[...] = jnp.zeros_like(au)

    def routed(ref, core, i):
        rows = pl.ds(pl.multiple_of(core * HALF_D + i * 640, 128), 640)
        ag[...] += mm(ref[i], wg[rows, :])
        au[...] += mm(ref[i], wu[rows, :])

    def own_part(i, _):
        routed(XO, c, i)
        return 0

    lax.fori_loop(0, 4, own_part, 0)
    for cp in x_cp:
        cp.wait_recv()

    def sib_part(i, _):
        routed(XR, 1 - c, i)
        return 0

    lax.fori_loop(0, 4, sib_part, 0)
    H[...] = (jax.nn.silu(ag[...]) * au[...]).astype(BF)

    for cp in h_cp:
        cp.wait_recv()
    rel = go(HT.at[c], HT.at[c], s_rel.at[0], r_rel.at[0], sibling)

    loads[5].wait()
    p_cp = []
    for g in range(3):
        w = pl.ds(0, WIDTH[g])
        PS[g, :, w] = mm(H[...], wd[:, half(1 - c, OFF[g], WIDTH[g])]).astype(BF)
        p_cp.append(go(PS.at[g, :, w], PR.at[g, :, w], s_p.at[g], r_p.at[g], sibling))

    rel.wait_recv()
    for t in range(2):
        part = mm(HT[t].reshape(384, 512), sdp, TN).astype(BF)
        for k in range(2):
            SD[2 * t + k] = part[256 * k : 256 * k + 256]
    sd_cp = []
    for d in (1, 2, 3):
        to = lax.rem(y + d, 4)
        sd_cp.append(go(SD.at[to], SDR.at[d - 1], s_sd.at[d - 1], r_sd.at[d - 1], peer(0, d)))

    for g in range(3):
        w = pl.ds(0, WIDTH[g])
        RO[g, :, w] = mm(H[...], wd[:, half(c, OFF[g], WIDTH[g])]).astype(BF)

    rs = {}
    for g in range(3):
        w = pl.ds(0, WIDTH[g])
        b3 = ORDERS[g][2]
        p_cp[g].wait_recv()
        both = (RO[g, :, w].astype(F32) + PR[g, :, w].astype(F32)).astype(BF)
        XC[g, :, :, w] = mm(GM[g], both).astype(BF).reshape(4, 64, WIDTH[g])
        for d in (1, 3, 2):
            to = lax.rem(pos[b3] + d, 4)
            rs[g, 0, d] = go(
                XC.at[g, to, :, w], RA.at[g, d, :, w], s_rs.at[g, 0, d - 1], r_rs.at[g, 0, d - 1], peer(b3, d)
            )
        RA[g, 0, :, w] = XC[g, pos[b3], :, w]

    for cp in sd_cp:
        cp.wait_recv()
    tot = SD[y].astype(F32)
    for d in range(3):
        tot = tot + SDR[d].astype(F32)
    tot = tot.astype(BF)
    SZ[0] = tot[:128]
    SZ[1] = tot[128:]
    z_cp = go(SZ.at[1 - zh], SZR, s_sd.at[3], r_sd.at[3], peer(1, 2))

    for g in range(3):
        w = pl.ds(0, WIDTH[g])
        _, b2, b3 = ORDERS[g]
        for d in (1, 3, 2):
            rs[g, 0, d].wait_recv()
        tot = mm(CT[g], RA[g, :, :, w].reshape(256, WIDTH[g]), TN)
        SA[g, :, :, :, w] = tot.astype(BF).reshape(4, 4, 16, WIDTH[g])
        first = min(a for a in range(3) if a != b3) == b2
        for d in (1, 3, 2):
            to = lax.rem(pos[b2] + d, 4)
            part = SA.at[g, to, :, :, w] if first else SA.at[g, :, to, :, w]
            rs[g, 1, d] = go(
                part, RB.at[g, d - 1, :, :, w], s_rs.at[g, 1, d - 1], r_rs.at[g, 1, d - 1], peer(b2, d)
            )

    z_cp.wait_recv()
    SQ[...] = (SZ[zh].astype(F32) + SZR[...].astype(F32)).astype(BF).reshape(8, 16, WIN)
    spread(SQ, SHR, s_q, r_q)

    for g in range(3):
        w = pl.ds(0, WIDTH[g])
        b1, b2, b3 = ORDERS[g]
        for d in (1, 3, 2):
            rs[g, 1, d].wait_recv()
        first = min(a for a in range(3) if a != b3) == b2
        tot = (SA[g, pos[b2], :, :, w] if first else SA[g, :, pos[b2], :, w]).astype(F32)
        for d in range(3):
            tot = tot + RB[g, d, :, :, w].astype(F32)
        SB[g, :, :, w] = tot.astype(BF)
        for d in (1, 3, 2):
            to = lax.rem(pos[b1] + d, 4)
            rs[g, 2, d] = go(
                SB.at[g, to, :, w], RC.at[g, d - 1, :, w], s_rs.at[g, 2, d - 1], r_rs.at[g, 2, d - 1], peer(b1, d)
            )

    spread_recv(SHR, r_q)
    SHA[...] = jnp.zeros_like(SHA)
    for j in range(4):
        for k in range(2):
            SHA[:, pl.ds(640 * j + 256 * k, WIN)] += SHR[j, k].astype(F32)
    f_cp = []
    for g in range(3):
        w = pl.ds(0, WIDTH[g])
        for d in (1, 3, 2):
            rs[g, 2, d].wait_recv()
        tot = SB[g, pos[ORDERS[g][0]], :, w].astype(F32) + SHA[:, pl.ds(OFF[g], WIDTH[g])]
        for d in range(3):
            tot = tot + RC[g, d, :, w].astype(F32)
        done = FO.at[:, half(c, OFF[g], WIDTH[g])]
        done[...] = tot.astype(BF)
        f_cp.append(go(done, done, s_f.at[g], r_f.at[g], sibling))
    for cp in f_cp:
        cp.wait_recv()
    res = FO[...].astype(F32)
    out[...] = jnp.where(c == 0, res[:8], res[8:]).astype(BF)
    for cp in pend:
        cp.wait_send()
    spread_end(WS, s_w)
    spread_end(SQ, s_q)


def local(tokens, gate_scores, expert_ids, expert_gate, expert_up, expert_down, shared_gate, shared_up, shared_down):
    vm, hbm = pl.BlockSpec(memory_space=pltpu.VMEM), pl.BlockSpec(memory_space=pl.ANY)

    def bf(*shape):
        return pltpu.VMEM(shape, BF)

    def f32(*shape):
        return pltpu.VMEM(shape, F32)

    def pair(*shape):
        return [pltpu.SemaphoreType.DMA(shape)] * 2

    return pl.pallas_call(
        kernel,
        out_shape=jax.ShapeDtypeStruct((8, D), BF),
        in_specs=[vm] * 3 + [hbm] * 6,
        out_specs=vm,
        scratch_shapes=[
            bf(4, 4, 4, 16, HALF_D), bf(4, 4, 4, 16, 128), bf(16, D), bf(16, HALF_D),
            f32(8, 128), bf(16, 128), bf(16, 128),
            bf(D, HALF), bf(D, HALF), bf(HALF, D), bf(320, 384), bf(320, 384), bf(320, 384),
            bf(8, 96, WIN), bf(4, 2, 96, WIN), bf(96, HALF_D),
            f32(96, 512), f32(96, 512), f32(96, 512), bf(2, 8, 48, 512),
            bf(256, 1024), bf(3, 256, 256), bf(3, 256, 256), bf(4, 256, 640), bf(4, 256, 640),
            f32(256, HALF), f32(256, HALF), bf(256, HALF),
            bf(3, 256, 896), bf(3, 256, 896), bf(3, 256, 896),
            bf(3, 4, 64, 896), bf(3, 4, 64, 896), bf(3, 4, 4, 16, 896), bf(3, 3, 4, 16, 896),
            bf(3, 4, 16, 896), bf(3, 3, 16, 896),
            bf(4, 256, WIN), bf(3, 256, WIN), bf(2, 128, WIN), bf(128, WIN), bf(8, 16, WIN),
            bf(4, 2, 16, WIN), f32(16, HALF_D), bf(16, D),
            pltpu.SemaphoreType.DMA((6,)),
            *pair(2), *pair(3, 3), *pair(3, 3), *pair(3, 3), *pair(3, 4, 6),
            pltpu.SemaphoreType.DMA((8,)), pltpu.SemaphoreType.DMA((4, 2)),
            *pair(1), *pair(4), *pair(7), *pair(1), *pair(3), *pair(4),
            pltpu.SemaphoreType.DMA((8,)), pltpu.SemaphoreType.DMA((4, 2)),
            *pair(3, 3, 3), *pair(3),
        ],
        compiler_params=pltpu.CompilerParams(
            collective_id=0, has_side_effects=True, vmem_limit_bytes=62 * 2**20
        ),
        cost_estimate=pl.CostEstimate(flops=13 * 10**9, bytes_accessed=25 * 10**6, transcendentals=10**6),
    )(
        tokens, gate_scores, expert_ids, expert_gate, expert_up, expert_down, shared_gate, shared_up, shared_down.T
    )


def solution(mesh):
    return jax.shard_map(
        local,
        mesh=mesh,
        in_specs=(
            P(("fsdp", "expert"), None),
            P(("fsdp", "expert"), None),
            P(("fsdp", "expert"), None),
            P(("fsdp", "expert"), None, None),
            P(("fsdp", "expert"), None, None),
            P(("fsdp", "expert"), None, None),
            P("expert", "fsdp"),
            P("expert", "fsdp"),
            P("fsdp", "expert"),
        ),
        out_specs=P(("fsdp", "expert"), None),
        check_vma=False,
    )
```

```python
import jax
import jax.numpy as jnp
from jax import lax
from jax.experimental import pallas as pl
from jax.experimental.pallas import tpu as pltpu
from jax.sharding import PartitionSpec as P

MESH = pl.DeviceIdType.MESH
BF, F32 = jnp.bfloat16, jnp.float32
D, HALF_D, HALF, WIN = 5120, 2560, 768, 384
ORDERS = ((0, 1, 2), (1, 2, 0), (2, 0, 1))
OFF, WIDTH = (0, 768, 1792), (768, 1024, 768)
ROFF, RWIDTH = (0, 1024, 1536), (1024, 512, 1024)
DAY = (256, 64, 16)
NN, TN, NT = (((1,), (0,)), ((), ())), (((0,), (0,)), ((), ())), (((1,), (1,)), ((), ()))


def mm(a, b, dims=NN):
    return lax.dot_general(a, b, dims, preferred_element_type=F32)


def running(v, width):
    lane = lax.broadcasted_iota(jnp.int32, v.shape, 1)
    step = 1
    while step < width:
        v = v + jnp.where(lane >= step, pltpu.roll(v, step, 1), 0.0)
        step *= 2
    return v


def kernel(
    tok, gates, ids, wg_h, wu_h, wd_h, sg_h, su_h, sd_h, out,
    T, ID, stage, sib, e8, idst, idsib, wg, wu, wd, sg, su, sd, WS, WR, WA, AC, SPR, HT,
    QF, QP, GM, CT, XP, XO, XR, ag, au, H, RO, PS, PR, XC, RA, SA, RB, SB, RC, SD, SDR, SZ, SZR, SQ, SHR, SHA, FO,
    lsem, s_sib, r_sib, s_id, r_id, s_a0, r_a0, s_a1, r_a1, s_a2, r_a2, s_w, r_w, s_sp, r_sp, s_x, r_x,
    s_h, r_h, s_rel, r_rel, s_p, r_p, s_sd, r_sd, s_q, r_q, s_rs, r_rs, s_f, r_f,
):
    f, e = lax.axis_index("fsdp"), lax.axis_index("expert")
    c = lax.rem(e, 2)
    y, x = f // 2, lax.rem(e // 2, 4)
    zh, zl = lax.rem(f, 2), e // 8
    pos = (y, zh * 2 + zl, x)
    chip = (y * 4 + pos[1]) * 4 + x
    mine = zl * 4 + x

    def dev(p, core):
        return (p[0] * 2 + p[1] // 2, (lax.rem(p[1], 2) * 4 + p[2]) * 2 + core)

    def peer(axis, dist):
        p = list(pos)
        p[axis] = lax.rem(p[axis] + dist, 4)
        return dev(p, c)

    def group(i):
        zz, xx = lax.rem(zl + i // 4, 2), lax.rem(x + i % 4, 4)
        return dev((y, zh * 2 + zz, xx), c), zz * 4 + xx

    def taker(i):
        zz, xx = lax.rem(zl + i // 4, 2), lax.rem(x + i % 4, 4)
        return dev((y, zh * 2 + zz, xx), zl), zz * 4 + xx

    def giver(i):
        return dev((y, zh * 2 + c, lax.rem(x + i % 4, 4)), lax.rem(c + i // 4, 2))

    sibling = dev(pos, 1 - c)

    def half(core, off, width):
        return pl.ds(pl.multiple_of(core * HALF_D + off, 128), width)

    def remote(src, dst, ss, rs, to):
        return pltpu.make_async_remote_copy(
            src_ref=src, dst_ref=dst, send_sem=ss, recv_sem=rs, device_id=to, device_id_type=MESH
        )

    pend = []

    def go(src, dst, ss, rs, to):
        cp = remote(src, dst, ss, rs, to)
        cp.start()
        pend.append(cp)
        return cp

    loads = [
        pltpu.make_async_copy(a, b, lsem.at[i])
        for i, (a, b) in enumerate(
            ((sg_h, sg), (su_h, su), (sd_h, sd), (wg_h.at[0], wg), (wu_h.at[0], wu), (wd_h.at[0], wd))
        )
    ]
    barrier = pltpu.get_barrier_semaphore()
    partners = [peer(a, d) for a in range(3) for d in (1, 2, 3)]
    partners += [group(i)[0] for i in (5, 6, 7)] + [sibling] + [giver(i) for i in range(1, 8)]
    for to in partners:
        pl.semaphore_signal(barrier, inc=1, device_id=to, device_id_type=MESH)

    @pl.when(zl != c)
    def _():
        pl.semaphore_signal(barrier, inc=1, device_id=giver(0), device_id_type=MESH)

    for ld in loads:
        ld.start()

    rows16 = lax.broadcasted_iota(jnp.int32, (16, 1), 0) // 8 == c
    v = tok[...].astype(F32)
    stage[...] = jnp.where(rows16, jnp.concatenate([v, v], 0), 0.0).astype(BF)
    e8[...] = jnp.full((8, 128), -1.0, F32)
    e8[:, pl.ds(0, 6)] = ids[...].astype(F32)
    e8[:, pl.ds(8, 6)] = gates[...].astype(F32)
    v = e8[...]
    idst[...] = jnp.where(rows16, jnp.concatenate([v, v], 0), 0.0).astype(BF)
    for ld in loads[:3]:
        ld.wait()
    k_at = lax.broadcasted_iota(jnp.int32, (320, WIN), 0)
    l_at = lax.broadcasted_iota(jnp.int32, (320, WIN), 1)
    shift = (l_at == k_at + 64 * c).astype(F32).astype(BF)
    wt = mm(sg[...], shift, TN).astype(BF)
    for j in range(8):
        WS[j, pl.ds(0, 48)] = wt[48 * j : 48 * j + 48]
    wt = mm(su[...], shift, TN).astype(BF)
    for j in range(8):
        WS[j, pl.ds(48, 48)] = wt[48 * j : 48 * j + 48]

    sdp = mm(sd[...], shift, TN).astype(BF)

    def spread(src, dst, ss, rs):
        for i in range(1, 8):
            to, j = taker(i)
            go(src.at[j], dst.at[x, c], ss.at[i], rs.at[i % 4, c], to)

        @pl.when(zl != c)
        def _():
            to, j = taker(0)
            remote(src.at[j], dst.at[x, c], ss.at[0], rs.at[0, c], to).start()

        @pl.when(zl == c)
        def _():
            dst[x, c] = src[mine]

    def spread_recv(dst, rs):
        for i in range(1, 8):
            cc = lax.rem(c + i // 4, 2)
            pltpu.make_async_copy(dst.at[0, 0], dst.at[0, 0], rs.at[i % 4, cc]).wait()

        @pl.when(zl != c)
        def _():
            pltpu.make_async_copy(dst.at[0, 0], dst.at[0, 0], rs.at[0, c]).wait()

    def spread_end(src, ss):
        @pl.when(zl != c)
        def _():
            pltpu.make_async_copy(src.at[0], src.at[0], ss.at[0]).wait()

    pl.semaphore_wait(barrier, len(partners) + jnp.where(zl != c, 1, 0))

    cp = go(idst, idsib, s_sib.at[0], r_sib.at[0], sibling)
    cp1 = go(stage.at[:, half(1 - c, 0, HALF_D)], sib, s_sib.at[1], r_sib.at[1], sibling)
    spread(WS, WR, s_w, r_w)

    def view(ref, order, depth, col):
        ix = [slice(None)] * 3
        for a in order[depth:]:
            ix[a] = pos[a]
        return ref.at[ix[0], ix[1], ix[2], :, col]

    def id_send(s):
        v = view(ID, (0, 1, 2), s, slice(None))
        return [go(v, v, s_id.at[s, d - 1], r_id.at[s, d - 1], peer(s, d)) for d in (1, 2, 3)]

    cp1.wait_recv()
    T[pos[0], pos[1], pos[2]] = stage[:, half(c, 0, HALF_D)] + sib[...]

    a0, a1, a2 = {}, {}, {}
    for g in range(3):
        v = view(T, ORDERS[g], 0, pl.ds(OFF[g], WIDTH[g]))
        for d in (1, 3, 2):
            a0[g, d] = go(v, v, s_a0.at[g, d - 1], r_a0.at[g, d - 1], peer(ORDERS[g][0], d))
    cp.wait_recv()
    ID[pos[0], pos[1], pos[2]] = idst[...] + idsib[...]
    id_cp = id_send(0)

    def piece(g, k, back, part):
        b1, b2, b3 = ORDERS[g]
        cut = 128 * ((WIDTH[g] // 128 + 1 - k % 2) // 2)
        ix = [slice(None)] * 3
        ix[b2] = lax.rem(pos[b2] + 4 - k, 4)
        ix[b3] = lax.rem(pos[b3] + 4 - back, 4)
        col = pl.ds(OFF[g], cut) if part == 0 else pl.ds(OFF[g] + cut, WIDTH[g] - cut)
        return T.at[ix[0], ix[1], ix[2], :, col]

    def third(g, k, j):
        back, part, way = ((0, 0, 1), (0, 1, 3), (0, 1, 1), (0, 0, 3), (1, 0, 1), (3, 1, 3))[j]
        v = piece(g, k, back, part)
        a2[g, k, j] = go(v, v, s_a2.at[g, k, j], r_a2.at[g, k, j], peer(ORDERS[g][2], way))

    def slab(g, k):
        for j in range(4):
            third(g, k, j)

    def pass_on(k):
        for g in range(3):
            for j in (0, 1):
                a2[g, k, j].wait_recv()
                third(g, k, j + 4)

    for g in range(3):
        for d in (1, 3, 2):
            a0[g, d].wait_recv()
        v = view(T, ORDERS[g], 1, pl.ds(OFF[g], WIDTH[g]))
        for d in (1, 3, 2):
            a1[g, d] = go(v, v, s_a1.at[g, d - 1], r_a1.at[g, d - 1], peer(ORDERS[g][1], d))
    for cp in id_cp:
        cp.wait_recv()
    id_cp = id_send(1)
    for g in range(3):
        slab(g, 0)

    for cp in id_cp:
        cp.wait_recv()
    id_cp = id_send(2)
    last = 0
    for k in (1, 3, 2):
        for g in range(3):
            a1[g, k].wait_recv()
            slab(g, k)
        pass_on(last)
        last = k
    pass_on(last)

    for cp in id_cp:
        cp.wait_recv()

    def ring_at(g, back):
        return lax.rem(pos[ORDERS[g][2]] + 4 - back, 4)

    def plane_ix(g, back):
        ix = [slice(None)] * 3
        ix[ORDERS[g][2]] = ring_at(g, back)
        return tuple(ix)

    def number(v):
        return v.astype(F32)

    def hits_of(info, expert):
        return (info[0:8] == number(expert)).astype(F32)

    def total(v):
        return jnp.sum(v, axis=0, keepdims=True)

    info = ID[...].reshape(1024, 128).astype(F32).T
    at = lax.broadcasted_iota(jnp.int32, (1, 1024), 1)
    hit = total(hits_of(info, chip))
    plane = [
        jnp.where(lax.rem(at // DAY[ORDERS[g][2]], 4) == ring_at(g, b), hit, 0.0) for g in range(3) for b in range(4)
    ]
    run = running(jnp.concatenate(plane + [hit] * 4, 0), 1024) - 1.0
    slot = lax.broadcasted_iota(jnp.int32, (64, 1024), 0).astype(F32)
    for g in range(3):
        for b in range(4):
            i = 4 * g + b
            QF[g, pl.ds(64 * b, 64)] = jnp.where(slot == run[i : i + 1], plane[i], 0.0).astype(BF)
    for g in (1, 2):
        GM[g - 1] = mm(QF[g], QF[0], NT).astype(BF)
    slot = lax.broadcasted_iota(jnp.int32, (64, 256), 0).astype(F32)
    for g in range(3):
        hits, weights, picks = [], [], []
        for b in range(4):
            info = ID[plane_ix(g, b)].reshape(256, 128).astype(F32).T
            picks.append(total(hits_of(info, chip)))
            if b == 0:
                for d in range(4):
                    p = list(pos)
                    p[ORDERS[g][2]] = ring_at(g, d)
                    eq = hits_of(info, (p[0] * 4 + p[1]) * 4 + p[2])
                    hits.append(total(eq))
                    weights.append(total(eq * info[8:16]))
        run = running(jnp.concatenate(hits + picks, 0), 256) - 1.0
        for d in range(4):
            CT[g, pl.ds(64 * d, 64)] = jnp.where(
                slot == run[d : d + 1], weights[d] * hits[d], 0.0
            ).astype(BF)
            QP[g, d] = jnp.where(slot == run[4 + d : 5 + d], picks[d], 0.0).astype(BF)

    spread_recv(WR, r_w)
    WA[...] = jnp.zeros_like(WA)
    for j in range(4):
        o = 640 * j
        for src, dst in ((0, 0), (48, 64)):
            r, w = pl.ds(src, 48), pl.ds(dst, 48)
            WA[w, pl.ds(o, 256)] = WR[j, 0, r, pl.ds(0, 256)]
            WA[w, pl.ds(o + 256, 128)] = WR[j, 0, r, pl.ds(256, 128)] + WR[j, 1, r, pl.ds(0, 128)]
            WA[w, pl.ds(o + 384, 256)] = WR[j, 1, r, pl.ds(128, 256)]

    AC[...] = jnp.zeros_like(AC)
    for b, js in ((0, ()), (1, (2,)), (3, (3,)), (2, (4, 5))):
        for g in range(3):
            for k in (0, 1, 3, 2):
                for j in js:
                    a2[g, k, j].wait_recv()
            ix, w, col = plane_ix(g, b), WIDTH[g], pl.ds(OFF[g], WIDTH[g])
            rows = T[(*ix, slice(None), col)].reshape(256, w)
            AC[ix] += mm(rows, WA[:, col], NT).reshape(4, 4, 16, 128)
            xp = mm(QP[g, b], rows).astype(BF)
            if g == 0:
                XO[pl.ds(64 * b, 64), col] = xp
            else:
                XP[g - 1, pl.ds(64 * b, 64), pl.ds(0, w)] = xp

    theirs = AC.at[pl.ds(2 * (1 - c), 2)]
    sp = go(theirs, SPR, s_sp.at[0], r_sp.at[0], sibling)

    x_cp = []
    for g in range(3):
        col = pl.ds(OFF[g], WIDTH[g])
        if g:
            XO[:, col] = mm(GM[g - 1], XP[g - 1, :, pl.ds(0, WIDTH[g])], TN).astype(BF)
        x_cp.append(go(XO.at[:, col], XR.at[:, col], s_x.at[g], r_x.at[g], sibling))

    loads[3].wait()
    loads[4].wait()
    ag[...] = jnp.zeros_like(ag)
    au[...] = jnp.zeros_like(au)

    def routed(ref, core, i):
        rows = pl.ds(pl.multiple_of(core * HALF_D + i * 512, 128), 512)
        part = ref[:, pl.ds(pl.multiple_of(i * 512, 128), 512)]
        ag[...] += mm(part, wg[rows, :])
        au[...] += mm(part, wu[rows, :])

    def own_part(i, _):
        routed(XO, c, i)
        return 0

    lax.fori_loop(0, 2, own_part, 0)
    sp.wait_recv()
    gu = (AC[pl.ds(2 * c, 2)] + SPR[...]).reshape(512, 128)
    hid = jax.nn.silu(gu) * pltpu.roll(gu, 64, 1)
    HT[c, mine] = hid.T[:48].astype(BF)
    h_cp = []
    for i in range(1, 8):
        to, j = group(i)
        h_cp.append(go(HT.at[c, mine], HT.at[c, mine], s_h.at[i - 1], r_h.at[i - 1], to))

    lax.fori_loop(2, 5, own_part, 0)
    for cp in x_cp:
        cp.wait_recv()

    def sib_part(i, _):
        routed(XR, 1 - c, i)
        return 0

    lax.fori_loop(0, 5, sib_part, 0)
    H[...] = (jax.nn.silu(ag[...]) * au[...]).astype(BF)
    for cp in h_cp:
        cp.wait_recv()
    rel = go(HT.at[c], HT.at[c], s_rel.at[0], r_rel.at[0], sibling)

    loads[5].wait()
    p_cp = []
    for g in range(3):
        w = pl.ds(0, RWIDTH[g])
        PS[g, :, w] = mm(H[...], wd[:, half(1 - c, ROFF[g], RWIDTH[g])]).astype(BF)
        p_cp.append(go(PS.at[g, :, w], PR.at[g, :, w], s_p.at[g], r_p.at[g], sibling))

    rel.wait_recv()
    for t in range(2):
        part = mm(HT[t].reshape(384, 512), sdp, TN).astype(BF)
        for k in range(2):
            SD[2 * t + k] = part[256 * k : 256 * k + 256]
    sd_cp = []
    for d in (1, 3, 2):
        to = lax.rem(y + d, 4)
        sd_cp.append(go(SD.at[to], SDR.at[d - 1], s_sd.at[d - 1], r_sd.at[d - 1], peer(0, d)))

    for g in range(3):
        w = pl.ds(0, RWIDTH[g])
        RO[g, :, w] = mm(H[...], wd[:, half(c, ROFF[g], RWIDTH[g])]).astype(BF)

    rs = {}
    for g in range(3):
        w = pl.ds(0, RWIDTH[g])
        b3 = ORDERS[g][2]
        p_cp[g].wait_recv()
        both = (RO[g, :, w].astype(F32) + PR[g, :, w].astype(F32)).astype(BF)
        if g:
            both = mm(GM[g - 1], both).astype(BF)
        XC[g, :, :, w] = both.reshape(4, 64, RWIDTH[g])
        for b in (3, 1, 2):
            rs[g, 0, b] = go(
                XC.at[g, b, :, w], RA.at[g, 4 - b, :, w], s_rs.at[g, 0, b - 1], r_rs.at[g, 0, b - 1], peer(b3, 4 - b)
            )
        RA[g, 0, :, w] = XC[g, 0, :, w]

    for cp in sd_cp:
        cp.wait_recv()
    tot = SD[y].astype(F32)
    for d in range(3):
        tot = tot + SDR[d].astype(F32)
    tot = tot.astype(BF)
    SZ[0] = tot[:128]
    SZ[1] = tot[128:]
    z_cp = go(SZ.at[1 - zh], SZR, s_sd.at[3], r_sd.at[3], peer(1, 2))

    z_cp.wait_recv()
    SQ[...] = (SZ[zh].astype(F32) + SZR[...].astype(F32)).astype(BF).reshape(8, 16, WIN)
    spread(SQ, SHR, s_q, r_q)

    for g in range(3):
        w = pl.ds(0, RWIDTH[g])
        _, b2, b3 = ORDERS[g]
        for d in (1, 3, 2):
            rs[g, 0, d].wait_recv()
        tot = mm(CT[g], RA[g, :, :, w].reshape(256, RWIDTH[g]), TN)
        SA[g, :, :, :, w] = tot.astype(BF).reshape(4, 4, 16, RWIDTH[g])
        first = min(a for a in range(3) if a != b3) == b2
        for d in (1, 3, 2):
            to = lax.rem(pos[b2] + d, 4)
            part = SA.at[g, to, :, :, w] if first else SA.at[g, :, to, :, w]
            rs[g, 1, d] = go(
                part, RB.at[g, d - 1, :, :, w], s_rs.at[g, 1, d - 1], r_rs.at[g, 1, d - 1], peer(b2, d)
            )

    for g in range(3):
        w = pl.ds(0, RWIDTH[g])
        b1, b2, b3 = ORDERS[g]
        for d in (1, 3, 2):
            rs[g, 1, d].wait_recv()
        first = min(a for a in range(3) if a != b3) == b2
        tot = (SA[g, pos[b2], :, :, w] if first else SA[g, :, pos[b2], :, w]).astype(F32)
        for d in range(3):
            tot = tot + RB[g, d, :, :, w].astype(F32)
        SB[g, :, :, w] = tot.astype(BF)
        for d in (1, 3, 2):
            to = lax.rem(pos[b1] + d, 4)
            rs[g, 2, d] = go(
                SB.at[g, to, :, w], RC.at[g, d - 1, :, w], s_rs.at[g, 2, d - 1], r_rs.at[g, 2, d - 1], peer(b1, d)
            )

    spread_recv(SHR, r_q)
    SHA[...] = jnp.zeros_like(SHA)
    for j in range(4):
        for k in range(2):
            SHA[:, pl.ds(640 * j + 256 * k, WIN)] += SHR[j, k].astype(F32)
    f_cp = []
    for g in range(3):
        w = pl.ds(0, RWIDTH[g])
        for d in (1, 3, 2):
            rs[g, 2, d].wait_recv()
        tot = SB[g, pos[ORDERS[g][0]], :, w].astype(F32) + SHA[:, pl.ds(ROFF[g], RWIDTH[g])]
        for d in range(3):
            tot = tot + RC[g, d, :, w].astype(F32)
        done = FO.at[:, half(c, ROFF[g], RWIDTH[g])]
        done[...] = tot.astype(BF)
        f_cp.append(go(done, done, s_f.at[g], r_f.at[g], sibling))
    for cp in f_cp:
        cp.wait_recv()
    res = FO[...].astype(F32)
    out[...] = jnp.where(c == 0, res[:8], res[8:]).astype(BF)
    for cp in pend:
        cp.wait_send()
    spread_end(WS, s_w)
    spread_end(SQ, s_q)


def local(tokens, gate_scores, expert_ids, expert_gate, expert_up, expert_down, shared_gate, shared_up, shared_down):
    vm, hbm = pl.BlockSpec(memory_space=pltpu.VMEM), pl.BlockSpec(memory_space=pl.ANY)

    def bf(*shape):
        return pltpu.VMEM(shape, BF)

    def f32(*shape):
        return pltpu.VMEM(shape, F32)

    def pair(*shape):
        return [pltpu.SemaphoreType.DMA(shape)] * 2

    return pl.pallas_call(
        kernel,
        out_shape=jax.ShapeDtypeStruct((8, D), BF),
        in_specs=[vm] * 3 + [hbm] * 6,
        out_specs=vm,
        scratch_shapes=[
            bf(4, 4, 4, 16, HALF_D), bf(4, 4, 4, 16, 128), bf(16, D), bf(16, HALF_D),
            f32(8, 128), bf(16, 128), bf(16, 128),
            bf(D, HALF), bf(D, HALF), bf(HALF, D), bf(320, 384), bf(320, 384), bf(320, 384),
            bf(8, 96, WIN), bf(4, 2, 96, WIN), bf(128, HALF_D),
            f32(4, 4, 4, 16, 128), f32(2, 4, 4, 16, 128), bf(2, 8, 48, 512),
            bf(3, 256, 1024), bf(3, 4, 64, 256), bf(2, 256, 256), bf(3, 256, 256),
            bf(2, 256, 1024), bf(256, HALF_D), bf(256, HALF_D),
            f32(256, HALF), f32(256, HALF), bf(256, HALF),
            bf(3, 256, 1024), bf(3, 256, 1024), bf(3, 256, 1024),
            bf(3, 4, 64, 1024), bf(3, 4, 64, 1024), bf(3, 4, 4, 16, 1024), bf(3, 3, 4, 16, 1024),
            bf(3, 4, 16, 1024), bf(3, 3, 16, 1024),
            bf(4, 256, WIN), bf(3, 256, WIN), bf(2, 128, WIN), bf(128, WIN), bf(8, 16, WIN),
            bf(4, 2, 16, WIN), f32(16, HALF_D), bf(16, D),
            pltpu.SemaphoreType.DMA((6,)),
            *pair(2), *pair(3, 3), *pair(3, 3), *pair(3, 3), *pair(3, 4, 6),
            pltpu.SemaphoreType.DMA((8,)), pltpu.SemaphoreType.DMA((4, 2)),
            *pair(1), *pair(3), *pair(7), *pair(1), *pair(3), *pair(4),
            pltpu.SemaphoreType.DMA((8,)), pltpu.SemaphoreType.DMA((4, 2)),
            *pair(3, 3, 3), *pair(3),
        ],
        compiler_params=pltpu.CompilerParams(
            collective_id=0, has_side_effects=True, vmem_limit_bytes=62 * 2**20
        ),
        cost_estimate=pl.CostEstimate(flops=13 * 10**9, bytes_accessed=25 * 10**6, transcendentals=10**6),
    )(
        tokens, gate_scores, expert_ids, expert_gate, expert_up, expert_down, shared_gate, shared_up, shared_down.T
    )


def solution(mesh):
    return jax.shard_map(
        local,
        mesh=mesh,
        in_specs=(
            P(("fsdp", "expert"), None),
            P(("fsdp", "expert"), None),
            P(("fsdp", "expert"), None),
            P(("fsdp", "expert"), None, None),
            P(("fsdp", "expert"), None, None),
            P(("fsdp", "expert"), None, None),
            P("expert", "fsdp"),
            P("expert", "fsdp"),
            P("fsdp", "expert"),
        ),
        out_specs=P(("fsdp", "expert"), None),
        check_vma=False,
    )
```

```python
import jax
import jax.numpy as jnp
from jax import lax
from jax.experimental import pallas as pl
from jax.experimental.pallas import tpu as pltpu
from jax.sharding import PartitionSpec as P

MESH = pl.DeviceIdType.MESH
BF, F32 = jnp.bfloat16, jnp.float32
D, HALF_D, HALF, WIN = 5120, 2560, 768, 384
ORDERS = ((0, 1, 2), (1, 2, 0), (2, 0, 1))
OFF, WIDTH = (0, 768, 1792), (768, 1024, 768)
ROFF, RWIDTH = (0, 1024, 1536), (1024, 512, 1024)
DAY = (256, 64, 16)
NN, TN, NT = (((1,), (0,)), ((), ())), (((0,), (0,)), ((), ())), (((1,), (1,)), ((), ()))


def mm(a, b, dims=NN):
    return lax.dot_general(a, b, dims, preferred_element_type=F32)


def running(v, width):
    lane = lax.broadcasted_iota(jnp.int32, v.shape, 1)
    step = 1
    while step < width:
        v = v + jnp.where(lane >= step, pltpu.roll(v, step, 1), 0.0)
        step *= 2
    return v


def kernel(
    tok, gates, ids, wg_h, wu_h, wd_h, sg_h, su_h, sd_h, out,
    T, ID, stage, sib, e8, idst, idsib, wg, wu, wd, sg, su, sd, WS, WR, WA, AC, SPR, HT,
    QF, QP, GM, CT, XP, XO, XR, ag, au, H, RO, PS, PR, XC, RA, SA, RB, SB, RC, SD, SDR, SZ, SZR, ZB, ZS, ZR, SQ, SHR, SHA, FO,
    lsem, s_sib, r_sib, s_id, r_id, s_a0, r_a0, s_a1, r_a1, s_a2, r_a2, s_w, r_w, s_sp, r_sp, s_x, r_x,
    s_h, r_h, s_rel, r_rel, s_p, r_p, s_sd, r_sd, s_q, r_q, s_rs, r_rs, s_f, r_f,
):
    f, e = lax.axis_index("fsdp"), lax.axis_index("expert")
    c = lax.rem(e, 2)
    y, x = f // 2, lax.rem(e // 2, 4)
    zh, zl = lax.rem(f, 2), e // 8
    pos = (y, zh * 2 + zl, x)
    chip = (y * 4 + pos[1]) * 4 + x
    mine = zl * 4 + x

    def dev(p, core):
        return (p[0] * 2 + p[1] // 2, (lax.rem(p[1], 2) * 4 + p[2]) * 2 + core)

    def peer(axis, dist):
        p = list(pos)
        p[axis] = lax.rem(p[axis] + dist, 4)
        return dev(p, c)

    def group(i):
        zz, xx = lax.rem(zl + i // 4, 2), lax.rem(x + i % 4, 4)
        return dev((y, zh * 2 + zz, xx), c), zz * 4 + xx

    def taker(i):
        zz, xx = lax.rem(zl + i // 4, 2), lax.rem(x + i % 4, 4)
        return dev((y, zh * 2 + zz, xx), zl), zz * 4 + xx

    def giver(i):
        return dev((y, zh * 2 + c, lax.rem(x + i % 4, 4)), lax.rem(c + i // 4, 2))

    sibling = dev(pos, 1 - c)

    def half(core, off, width):
        return pl.ds(pl.multiple_of(core * HALF_D + off, 128), width)

    def remote(src, dst, ss, rs, to):
        return pltpu.make_async_remote_copy(
            src_ref=src, dst_ref=dst, send_sem=ss, recv_sem=rs, device_id=to, device_id_type=MESH
        )

    pend = []

    def go(src, dst, ss, rs, to):
        cp = remote(src, dst, ss, rs, to)
        cp.start()
        pend.append(cp)
        return cp

    loads = [
        pltpu.make_async_copy(a, b, lsem.at[i])
        for i, (a, b) in enumerate(
            ((sg_h, sg), (su_h, su), (sd_h, sd), (wg_h.at[0], wg), (wu_h.at[0], wu), (wd_h.at[0], wd))
        )
    ]
    barrier = pltpu.get_barrier_semaphore()
    partners = [peer(a, d) for a in range(3) for d in (1, 2, 3)]
    partners += [group(i)[0] for i in (5, 6, 7)] + [sibling] + [giver(i) for i in range(1, 8)]
    for to in partners:
        pl.semaphore_signal(barrier, inc=1, device_id=to, device_id_type=MESH)

    @pl.when(zl != c)
    def _():
        pl.semaphore_signal(barrier, inc=1, device_id=giver(0), device_id_type=MESH)

    for ld in loads:
        ld.start()

    rows16 = lax.broadcasted_iota(jnp.int32, (16, 1), 0) // 8 == c
    v = tok[...].astype(F32)
    stage[...] = jnp.where(rows16, jnp.concatenate([v, v], 0), 0.0).astype(BF)
    e8[...] = jnp.full((8, 128), -1.0, F32)
    e8[:, pl.ds(0, 6)] = ids[...].astype(F32)
    e8[:, pl.ds(8, 6)] = gates[...].astype(F32)
    v = e8[...]
    idst[...] = jnp.where(rows16, jnp.concatenate([v, v], 0), 0.0).astype(BF)
    for ld in loads[:3]:
        ld.wait()
    k_at = lax.broadcasted_iota(jnp.int32, (320, WIN), 0)
    l_at = lax.broadcasted_iota(jnp.int32, (320, WIN), 1)
    shift = (l_at == k_at + 64 * c).astype(F32).astype(BF)
    wt = mm(sg[...], shift, TN).astype(BF)
    for j in range(8):
        WS[j, pl.ds(0, 48)] = wt[48 * j : 48 * j + 48]
    wt = mm(su[...], shift, TN).astype(BF)
    for j in range(8):
        WS[j, pl.ds(48, 48)] = wt[48 * j : 48 * j + 48]

    sdp = mm(sd[...], shift, TN).astype(BF)

    def spread(src, dst, ss, rs):
        for i in range(1, 8):
            to, j = taker(i)
            go(src.at[j], dst.at[x, c], ss.at[i], rs.at[i % 4, c], to)

        @pl.when(zl != c)
        def _():
            to, j = taker(0)
            remote(src.at[j], dst.at[x, c], ss.at[0], rs.at[0, c], to).start()

        @pl.when(zl == c)
        def _():
            dst[x, c] = src[mine]

    def spread_recv(dst, rs):
        for i in range(1, 8):
            cc = lax.rem(c + i // 4, 2)
            pltpu.make_async_copy(dst.at[0, 0], dst.at[0, 0], rs.at[i % 4, cc]).wait()

        @pl.when(zl != c)
        def _():
            pltpu.make_async_copy(dst.at[0, 0], dst.at[0, 0], rs.at[0, c]).wait()

    def spread_end(src, ss):
        @pl.when(zl != c)
        def _():
            pltpu.make_async_copy(src.at[0], src.at[0], ss.at[0]).wait()

    pl.semaphore_wait(barrier, len(partners) + jnp.where(zl != c, 1, 0))

    cp = go(idst, idsib, s_sib.at[0], r_sib.at[0], sibling)
    cp1 = go(stage.at[:, half(1 - c, 0, HALF_D)], sib, s_sib.at[1], r_sib.at[1], sibling)
    spread(WS, WR, s_w, r_w)

    def view(ref, order, depth, col):
        ix = [slice(None)] * 3
        for a in order[depth:]:
            ix[a] = pos[a]
        return ref.at[ix[0], ix[1], ix[2], :, col]

    def id_send(s):
        v = view(ID, (0, 1, 2), s, slice(None))
        return [go(v, v, s_id.at[s, d - 1], r_id.at[s, d - 1], peer(s, d)) for d in (1, 2, 3)]

    cp1.wait_recv()
    T[pos[0], pos[1], pos[2]] = stage[:, half(c, 0, HALF_D)] + sib[...]

    a0, a1, a2 = {}, {}, {}
    for g in range(3):
        v = view(T, ORDERS[g], 0, pl.ds(OFF[g], WIDTH[g]))
        for d in (1, 3, 2):
            a0[g, d] = go(v, v, s_a0.at[g, d - 1], r_a0.at[g, d - 1], peer(ORDERS[g][0], d))
    cp.wait_recv()
    ID[pos[0], pos[1], pos[2]] = idst[...] + idsib[...]
    id_cp = id_send(0)

    def piece(g, k, back, part):
        b1, b2, b3 = ORDERS[g]
        cut = 128 * ((WIDTH[g] // 128 + 1 - k % 2) // 2)
        ix = [slice(None)] * 3
        ix[b2] = lax.rem(pos[b2] + 4 - k, 4)
        ix[b3] = lax.rem(pos[b3] + 4 - back, 4)
        col = pl.ds(OFF[g], cut) if part == 0 else pl.ds(OFF[g] + cut, WIDTH[g] - cut)
        return T.at[ix[0], ix[1], ix[2], :, col]

    def third(g, k, j):
        back, part, way = ((0, 0, 1), (0, 1, 3), (0, 1, 1), (0, 0, 3), (1, 0, 1), (3, 1, 3))[j]
        v = piece(g, k, back, part)
        a2[g, k, j] = go(v, v, s_a2.at[g, k, j], r_a2.at[g, k, j], peer(ORDERS[g][2], way))

    def slab(g, k):
        for j in range(4):
            third(g, k, j)

    def pass_on(k):
        for g in range(3):
            for j in (0, 1):
                a2[g, k, j].wait_recv()
                third(g, k, j + 4)

    for g in range(3):
        for d in (1, 3, 2):
            a0[g, d].wait_recv()
        v = view(T, ORDERS[g], 1, pl.ds(OFF[g], WIDTH[g]))
        for d in (1, 3, 2):
            a1[g, d] = go(v, v, s_a1.at[g, d - 1], r_a1.at[g, d - 1], peer(ORDERS[g][1], d))
    for cp in id_cp:
        cp.wait_recv()
    id_cp = id_send(1)
    for g in range(3):
        slab(g, 0)

    for cp in id_cp:
        cp.wait_recv()
    id_cp = id_send(2)
    last = 0
    for k in (1, 3, 2):
        for g in range(3):
            a1[g, k].wait_recv()
            slab(g, k)
        pass_on(last)
        last = k
    pass_on(last)

    for cp in id_cp:
        cp.wait_recv()

    def ring_at(g, back):
        return lax.rem(pos[ORDERS[g][2]] + 4 - back, 4)

    def plane_ix(g, back):
        ix = [slice(None)] * 3
        ix[ORDERS[g][2]] = ring_at(g, back)
        return tuple(ix)

    def number(v):
        return v.astype(F32)

    def hits_of(info, expert):
        return (info[0:8] == number(expert)).astype(F32)

    def total(v):
        return jnp.sum(v, axis=0, keepdims=True)

    info = ID[...].reshape(1024, 128).astype(F32).T
    at = lax.broadcasted_iota(jnp.int32, (1, 1024), 1)
    hit = total(hits_of(info, chip))
    plane = [
        jnp.where(lax.rem(at // DAY[ORDERS[g][2]], 4) == ring_at(g, b), hit, 0.0) for g in range(3) for b in range(4)
    ]
    run = running(jnp.concatenate(plane + [hit] * 4, 0), 1024) - 1.0
    slot = lax.broadcasted_iota(jnp.int32, (64, 1024), 0).astype(F32)
    for g in range(3):
        for b in range(4):
            i = 4 * g + b
            QF[g, pl.ds(64 * b, 64)] = jnp.where(slot == run[i : i + 1], plane[i], 0.0).astype(BF)
    for g in (1, 2):
        GM[g - 1] = mm(QF[g], QF[0], NT).astype(BF)
    slot = lax.broadcasted_iota(jnp.int32, (64, 256), 0).astype(F32)
    for g in range(3):
        hits, weights, picks = [], [], []
        for b in range(4):
            info = ID[plane_ix(g, b)].reshape(256, 128).astype(F32).T
            picks.append(total(hits_of(info, chip)))
            if b == 0:
                for d in range(4):
                    p = list(pos)
                    p[ORDERS[g][2]] = ring_at(g, d)
                    eq = hits_of(info, (p[0] * 4 + p[1]) * 4 + p[2])
                    hits.append(total(eq))
                    weights.append(total(eq * info[8:16]))
        run = running(jnp.concatenate(hits + picks, 0), 256) - 1.0
        for d in range(4):
            CT[g, pl.ds(64 * d, 64)] = jnp.where(
                slot == run[d : d + 1], weights[d] * hits[d], 0.0
            ).astype(BF)
            QP[g, d] = jnp.where(slot == run[4 + d : 5 + d], picks[d], 0.0).astype(BF)

    spread_recv(WR, r_w)
    WA[...] = jnp.zeros_like(WA)
    for j in range(4):
        o = 640 * j
        for src, dst in ((0, 0), (48, 64)):
            r, w = pl.ds(src, 48), pl.ds(dst, 48)
            WA[w, pl.ds(o, 256)] = WR[j, 0, r, pl.ds(0, 256)]
            WA[w, pl.ds(o + 256, 128)] = WR[j, 0, r, pl.ds(256, 128)] + WR[j, 1, r, pl.ds(0, 128)]
            WA[w, pl.ds(o + 384, 256)] = WR[j, 1, r, pl.ds(128, 256)]

    AC[...] = jnp.zeros_like(AC)
    for b, js in ((0, ()), (1, (2,)), (3, (3,)), (2, (4, 5))):
        for g in range(3):
            for k in (0, 1, 3, 2):
                for j in js:
                    a2[g, k, j].wait_recv()
            ix, w, col = plane_ix(g, b), WIDTH[g], pl.ds(OFF[g], WIDTH[g])
            rows = T[(*ix, slice(None), col)].reshape(256, w)
            AC[ix] += mm(rows, WA[:, col], NT).reshape(4, 4, 16, 128)
            xp = mm(QP[g, b], rows).astype(BF)
            if g == 0:
                XO[pl.ds(64 * b, 64), col] = xp
            else:
                XP[g - 1, pl.ds(64 * b, 64), pl.ds(0, w)] = xp

    theirs = AC.at[pl.ds(2 * (1 - c), 2)]
    sp = go(theirs, SPR, s_sp.at[0], r_sp.at[0], sibling)

    x_cp = []
    for g in range(3):
        col = pl.ds(OFF[g], WIDTH[g])
        if g:
            XO[:, col] = mm(GM[g - 1], XP[g - 1, :, pl.ds(0, WIDTH[g])], TN).astype(BF)
        x_cp.append(go(XO.at[:, col], XR.at[:, col], s_x.at[g], r_x.at[g], sibling))

    loads[3].wait()
    loads[4].wait()
    ag[...] = jnp.zeros_like(ag)
    au[...] = jnp.zeros_like(au)

    def routed(ref, core, i):
        rows = pl.ds(pl.multiple_of(core * HALF_D + i * 512, 128), 512)
        part = ref[:, pl.ds(pl.multiple_of(i * 512, 128), 512)]
        ag[...] += mm(part, wg[rows, :])
        au[...] += mm(part, wu[rows, :])

    def own_part(i, _):
        routed(XO, c, i)
        return 0

    lax.fori_loop(0, 2, own_part, 0)
    sp.wait_recv()
    gu = (AC[pl.ds(2 * c, 2)] + SPR[...]).reshape(512, 128)
    hid = jax.nn.silu(gu) * pltpu.roll(gu, 64, 1)
    HT[c, mine] = hid.T[:48].astype(BF)
    h_cp = []
    for i in range(1, 8):
        to, j = group(i)
        h_cp.append(go(HT.at[c, mine], HT.at[c, mine], s_h.at[i - 1], r_h.at[i - 1], to))

    lax.fori_loop(2, 5, own_part, 0)
    for cp in x_cp:
        cp.wait_recv()

    def sib_part(i, _):
        routed(XR, 1 - c, i)
        return 0

    lax.fori_loop(0, 5, sib_part, 0)
    H[...] = (jax.nn.silu(ag[...]) * au[...]).astype(BF)
    for cp in h_cp:
        cp.wait_recv()
    rel = go(HT.at[c], HT.at[c], s_rel.at[0], r_rel.at[0], sibling)

    LOW, TOP = pl.ds(0, 256), pl.ds(256, 128)

    def z_rows(at):
        return pl.ds(pl.multiple_of(at * 128, 128), 128)

    loads[5].wait()
    p_cp = []
    for g in range(3):
        w = pl.ds(0, RWIDTH[g])
        PS[g, :, w] = mm(H[...], wd[:, half(1 - c, ROFF[g], RWIDTH[g])]).astype(BF)
        p_cp.append(go(PS.at[g, :, w], PR.at[g, :, w], s_p.at[g], r_p.at[g], sibling))

    rel.wait_recv()
    for t in range(2):
        part = mm(HT[t].reshape(384, 512), sdp, TN).astype(BF)
        for k in range(2):
            SD[2 * t + k] = part[256 * k : 256 * k + 256]
    zb = go(SD.at[:, z_rows(1 - zh), TOP], ZB, s_sd.at[4], r_sd.at[4], peer(1, 2))
    sd_cp = []
    for d in (1, 3, 2):
        to = lax.rem(y + d, 4)
        sd_cp.append(
            go(SD.at[to, :, LOW], SDR.at[d - 1, :, LOW], s_sd.at[d - 1], r_sd.at[d - 1], peer(0, d))
        )

    for g in range(3):
        w = pl.ds(0, RWIDTH[g])
        RO[g, :, w] = mm(H[...], wd[:, half(c, ROFF[g], RWIDTH[g])]).astype(BF)

    rs = {}
    for g in range(3):
        w = pl.ds(0, RWIDTH[g])
        b3 = ORDERS[g][2]
        p_cp[g].wait_recv()
        both = (RO[g, :, w].astype(F32) + PR[g, :, w].astype(F32)).astype(BF)
        if g:
            both = mm(GM[g - 1], both).astype(BF)
        XC[g, :, :, w] = both.reshape(4, 64, RWIDTH[g])
        for b in (3, 1, 2):
            rs[g, 0, b] = go(
                XC.at[g, b, :, w], RA.at[g, 4 - b, :, w], s_rs.at[g, 0, b - 1], r_rs.at[g, 0, b - 1], peer(b3, 4 - b)
            )
        RA[g, 0, :, w] = XC[g, 0, :, w]

    zb.wait_recv()
    ZS[...] = (SD[:, z_rows(zh), TOP].astype(F32) + ZB[...].astype(F32)).astype(BF)
    zy = []
    for d in (1, 3, 2):
        to = lax.rem(y + d, 4)
        zy.append(go(ZS.at[to], ZR.at[d - 1], s_sd.at[4 + d], r_sd.at[4 + d], peer(0, d)))

    for cp in sd_cp:
        cp.wait_recv()
    tot = SD[y, :, LOW].astype(F32)
    for d in range(3):
        tot = tot + SDR[d, :, LOW].astype(F32)
    tot = tot.astype(BF)
    SZ[0] = tot[:128]
    SZ[1] = tot[128:]
    z_cp = go(SZ.at[1 - zh], SZR, s_sd.at[3], r_sd.at[3], peer(1, 2))

    z_cp.wait_recv()
    SQ[:, :, LOW] = (SZ[zh].astype(F32) + SZR[...].astype(F32)).astype(BF).reshape(8, 16, 256)
    for cp in zy:
        cp.wait_recv()
    tot = ZS[y].astype(F32)
    for d in range(3):
        tot = tot + ZR[d].astype(F32)
    SQ[:, :, TOP] = tot.astype(BF).reshape(8, 16, 128)
    spread(SQ, SHR, s_q, r_q)

    for g in range(3):
        w = pl.ds(0, RWIDTH[g])
        _, b2, b3 = ORDERS[g]
        for d in (1, 3, 2):
            rs[g, 0, d].wait_recv()
        tot = mm(CT[g], RA[g, :, :, w].reshape(256, RWIDTH[g]), TN)
        SA[g, :, :, :, w] = tot.astype(BF).reshape(4, 4, 16, RWIDTH[g])
        first = min(a for a in range(3) if a != b3) == b2
        for d in (1, 3, 2):
            to = lax.rem(pos[b2] + d, 4)
            part = SA.at[g, to, :, :, w] if first else SA.at[g, :, to, :, w]
            rs[g, 1, d] = go(
                part, RB.at[g, d - 1, :, :, w], s_rs.at[g, 1, d - 1], r_rs.at[g, 1, d - 1], peer(b2, d)
            )

    for g in range(3):
        w = pl.ds(0, RWIDTH[g])
        b1, b2, b3 = ORDERS[g]
        for d in (1, 3, 2):
            rs[g, 1, d].wait_recv()
        first = min(a for a in range(3) if a != b3) == b2
        tot = (SA[g, pos[b2], :, :, w] if first else SA[g, :, pos[b2], :, w]).astype(F32)
        for d in range(3):
            tot = tot + RB[g, d, :, :, w].astype(F32)
        SB[g, :, :, w] = tot.astype(BF)
        for d in (1, 3, 2):
            to = lax.rem(pos[b1] + d, 4)
            rs[g, 2, d] = go(
                SB.at[g, to, :, w], RC.at[g, d - 1, :, w], s_rs.at[g, 2, d - 1], r_rs.at[g, 2, d - 1], peer(b1, d)
            )

    spread_recv(SHR, r_q)
    SHA[...] = jnp.zeros_like(SHA)
    for j in range(4):
        for k in range(2):
            SHA[:, pl.ds(640 * j + 256 * k, WIN)] += SHR[j, k].astype(F32)
    f_cp = []
    for g in range(3):
        w = pl.ds(0, RWIDTH[g])
        for d in (1, 3, 2):
            rs[g, 2, d].wait_recv()
        tot = SB[g, pos[ORDERS[g][0]], :, w].astype(F32) + SHA[:, pl.ds(ROFF[g], RWIDTH[g])]
        for d in range(3):
            tot = tot + RC[g, d, :, w].astype(F32)
        done = FO.at[:, half(c, ROFF[g], RWIDTH[g])]
        done[...] = tot.astype(BF)
        f_cp.append(go(done, done, s_f.at[g], r_f.at[g], sibling))
    for cp in f_cp:
        cp.wait_recv()
    res = FO[...].astype(F32)
    out[...] = jnp.where(c == 0, res[:8], res[8:]).astype(BF)
    for cp in pend:
        cp.wait_send()
    spread_end(WS, s_w)
    spread_end(SQ, s_q)


def local(tokens, gate_scores, expert_ids, expert_gate, expert_up, expert_down, shared_gate, shared_up, shared_down):
    vm, hbm = pl.BlockSpec(memory_space=pltpu.VMEM), pl.BlockSpec(memory_space=pl.ANY)

    def bf(*shape):
        return pltpu.VMEM(shape, BF)

    def f32(*shape):
        return pltpu.VMEM(shape, F32)

    def pair(*shape):
        return [pltpu.SemaphoreType.DMA(shape)] * 2

    return pl.pallas_call(
        kernel,
        out_shape=jax.ShapeDtypeStruct((8, D), BF),
        in_specs=[vm] * 3 + [hbm] * 6,
        out_specs=vm,
        scratch_shapes=[
            bf(4, 4, 4, 16, HALF_D), bf(4, 4, 4, 16, 128), bf(16, D), bf(16, HALF_D),
            f32(8, 128), bf(16, 128), bf(16, 128),
            bf(D, HALF), bf(D, HALF), bf(HALF, D), bf(320, 384), bf(320, 384), bf(320, 384),
            bf(8, 96, WIN), bf(4, 2, 96, WIN), bf(128, HALF_D),
            f32(4, 4, 4, 16, 128), f32(2, 4, 4, 16, 128), bf(2, 8, 48, 512),
            bf(3, 256, 1024), bf(3, 4, 64, 256), bf(2, 256, 256), bf(3, 256, 256),
            bf(2, 256, 1024), bf(256, HALF_D), bf(256, HALF_D),
            f32(256, HALF), f32(256, HALF), bf(256, HALF),
            bf(3, 256, 1024), bf(3, 256, 1024), bf(3, 256, 1024),
            bf(3, 4, 64, 1024), bf(3, 4, 64, 1024), bf(3, 4, 4, 16, 1024), bf(3, 3, 4, 16, 1024),
            bf(3, 4, 16, 1024), bf(3, 3, 16, 1024),
            bf(4, 256, WIN), bf(3, 256, WIN), bf(2, 128, 256), bf(128, 256), bf(4, 128, 128), bf(4, 128, 128), bf(3, 128, 128), bf(8, 16, WIN),
            bf(4, 2, 16, WIN), f32(16, HALF_D), bf(16, D),
            pltpu.SemaphoreType.DMA((6,)),
            *pair(2), *pair(3, 3), *pair(3, 3), *pair(3, 3), *pair(3, 4, 6),
            pltpu.SemaphoreType.DMA((8,)), pltpu.SemaphoreType.DMA((4, 2)),
            *pair(1), *pair(3), *pair(7), *pair(1), *pair(3), *pair(8),
            pltpu.SemaphoreType.DMA((8,)), pltpu.SemaphoreType.DMA((4, 2)),
            *pair(3, 3, 3), *pair(3),
        ],
        compiler_params=pltpu.CompilerParams(
            collective_id=0, has_side_effects=True, vmem_limit_bytes=62 * 2**20
        ),
        cost_estimate=pl.CostEstimate(flops=13 * 10**9, bytes_accessed=25 * 10**6, transcendentals=10**6),
    )(
        tokens, gate_scores, expert_ids, expert_gate, expert_up, expert_down, shared_gate, shared_up, shared_down.T
    )


def solution(mesh):
    return jax.shard_map(
        local,
        mesh=mesh,
        in_specs=(
            P(("fsdp", "expert"), None),
            P(("fsdp", "expert"), None),
            P(("fsdp", "expert"), None),
            P(("fsdp", "expert"), None, None),
            P(("fsdp", "expert"), None, None),
            P(("fsdp", "expert"), None, None),
            P("expert", "fsdp"),
            P("expert", "fsdp"),
            P("fsdp", "expert"),
        ),
        out_specs=P(("fsdp", "expert"), None),
        check_vma=False,
    )
```
